128 devices in a mesh: wide: 32 (over x, y, core), narrow: 4 (over z).
Axes of the slice: x: 4, y: 4, z: 4, core: 2. Of those that a mesh axis runs over, the one named last changes fastest.
Arguments:
- tokens: bfloat16 [16384, 768], P('wide'), may hold values from -6 to 6
- memory: bfloat16 [16384, 768], P('wide'), may hold values from -6 to 6
- cotangent: bfloat16 [16384, 768], P('wide'), may hold values from -7.2 to 7.2
- lengths: int32 [256], P('wide'), may hold values from 1 to 256, as said below
- memory_lengths: int32 [256], P('wide'), may hold values from 1 to 64, as said below
- self_weight: float32 [3, 768, 768], P(None, 'wide', 'narrow'), may hold values from -0.21875 to 0.21875
- self_moment: float32 [3, 768, 768], P(None, 'wide', 'narrow'), may hold values from -0.00021362305 to 0.00021362305
- self_square: float32 [3, 768, 768], P(None, 'wide', 'narrow'), may hold values from 1.0593364e-10 to 4.2373455e-10
- cross_weight: float32 [3, 768, 768], P(None, 'wide', 'narrow'), may hold values from -0.21875 to 0.21875
- cross_moment: float32 [3, 768, 768], P(None, 'wide', 'narrow'), may hold values from -0.00021362305 to 0.00021362305
- cross_square: float32 [3, 768, 768], P(None, 'wide', 'narrow'), may hold values from 1.0593364e-10 to 4.2373455e-10
- merge_weight: float32 [2, 768, 768], P(None, 'narrow', 'wide'), may hold values from -0.625 to 0.625
- merge_moment: float32 [2, 768, 768], P(None, 'narrow', 'wide'), may hold values from -0.00021362305 to 0.00021362305
- merge_square: float32 [2, 768, 768], P(None, 'narrow', 'wide'), may hold values from 1.0593364e-10 to 4.2373455e-10
- expand_weight: float32 [768, 3072], P('wide', 'narrow'), may hold values from -0.21875 to 0.21875
- expand_moment: float32 [768, 3072], P('wide', 'narrow'), may hold values from -0.00021362305 to 0.00021362305
- expand_square: float32 [768, 3072], P('wide', 'narrow'), may hold values from 1.0593364e-10 to 4.2373455e-10
- shrink_weight: float32 [3072, 768], P('narrow', 'wide'), may hold values from -0.109375 to 0.109375
- shrink_moment: float32 [3072, 768], P('narrow', 'wide'), may hold values from -0.00021362305 to 0.00021362305
- shrink_square: float32 [3072, 768], P('narrow', 'wide'), may hold values from 1.0593364e-10 to 4.2373455e-10
- norm_gains: float32 [3, 768], P(None, 'wide'), may hold values from 0.28 to 2.84
- gains_moment: float32 [3, 768], P(None, 'wide'), may hold values from -0.0012207031 to 0.0012207031
- gains_square: float32 [3, 768], P(None, 'wide'), may hold values from 3.1780092e-09 to 1.2712037e-08
- bucket_bias: float32 [12, 32], P('narrow', 'wide'), may hold values from -4 to 4
- bias_moment: float32 [12, 32], P('narrow', 'wide'), may hold values from -0.0012207031 to 0.0012207031
- bias_square: float32 [12, 32], P('narrow', 'wide'), may hold values from 3.1780092e-09 to 1.2712037e-08
Outputs:
- layer_output: bfloat16 [16384, 768], P('wide')
- tokens_gradient: float32 [16384, 768], P('wide')
- memory_gradient: float32 [16384, 768], P('wide')
- gradient_norm: float32 [], replicated
- self_next: float32 [3, 768, 768], P(None, 'wide', 'narrow')
- self_moment_next: float32 [3, 768, 768], P(None, 'wide', 'narrow')
- self_square_next: float32 [3, 768, 768], P(None, 'wide', 'narrow')
- cross_next: float32 [3, 768, 768], P(None, 'wide', 'narrow')
- cross_moment_next: float32 [3, 768, 768], P(None, 'wide', 'narrow')
- cross_square_next: float32 [3, 768, 768], P(None, 'wide', 'narrow')
- merge_next: float32 [2, 768, 768], P(None, 'narrow', 'wide')
- merge_moment_next: float32 [2, 768, 768], P(None, 'narrow', 'wide')
- merge_square_next: float32 [2, 768, 768], P(None, 'narrow', 'wide')
- expand_next: float32 [768, 3072], P('wide', 'narrow')
- expand_moment_next: float32 [768, 3072], P('wide', 'narrow')
- expand_square_next: float32 [768, 3072], P('wide', 'narrow')
- shrink_next: float32 [3072, 768], P('narrow', 'wide')
- shrink_moment_next: float32 [3072, 768], P('narrow', 'wide')
- shrink_square_next: float32 [3072, 768], P('narrow', 'wide')
- gains_next: float32 [3, 768], P(None, 'wide')
- gains_moment_next: float32 [3, 768], P(None, 'wide')
- gains_square_next: float32 [3, 768], P(None, 'wide')
- bias_next: float32 [12, 32], P('narrow', 'wide')
- bias_moment_next: float32 [12, 32], P('narrow', 'wide')
- bias_square_next: float32 [12, 32], P('narrow', 'wide')
The draws below stay inside these ranges and needn't reach their ends.
Inputs may be any that keep to these rules, and one draw needn't show every extreme that they name: The 8 lengths of one index of wide sum to at most 512; each index of wide has one sequence of 128 to 256 tokens, the others have at most 36. `memory_lengths`: the 8 lengths of one index of wide sum to at most 512.
All inputs are finite; a program needn't handle non-finite values.
Results may differ from the reference program's by a relative error of at most 0.018.
The reference program's roundings to bfloat16 on the way count: a program that leaves them out, or rounds other values in their place, can miss the bound.
Values may be sent and summed in bfloat16 or wider, within the bound.
A program may use at most 128 MiB of HBM per device.

```python
import math
import jax
import jax.numpy as jnp
from jax import lax

D = 768
H = 12
HD = 64
FF = 3072
NB = 32
TOK = 512
DOCS = 8
STEP = 10
LMAX = 256
SHORT = 36
ELEN = 64
TOKENS = 16384
DOCS_ALL = 256
PARAMS = 9439872
N_WIDE = 32


def draw_norm_gains(key, part):
    key = jax.random.fold_in(key, 11)
    column = jnp.arange(D, dtype=jnp.float32) / (D - 1)
    ramp = 0.6 * 3.0 ** column
    noise = jnp.exp(jax.random.uniform(key, (3, D), jnp.float32, -0.35, 0.35))
    return ramp[None, :] * noise


def draw_cotangent(key, part):
    key = jax.random.fold_in(key, 12)
    column = jnp.arange(D, dtype=jnp.float32) / (D - 1)
    ramp = 0.6 * 3.0 ** column
    base = jax.random.truncated_normal(key, -4.0, 4.0, (TOKENS, D), jnp.float32)
    return (base * ramp[None, :]).astype(jnp.bfloat16)


def draw_lengths(key, part):
    key = jax.random.fold_in(key, 13)
    shards = DOCS_ALL // DOCS
    short_key, long_key, pick_key, top_key = jax.random.split(key, 4)
    short = jax.random.randint(short_key, (shards, DOCS), 1, SHORT + 1)
    long_len = jax.random.randint(long_key, (shards,), LMAX // 2, LMAX + 1)
    chosen = jax.random.randint(pick_key, (shards,), 0, DOCS)
    top_shard = jax.random.randint(top_key, (), 0, shards)
    long_len = jnp.where(jnp.arange(shards) == top_shard, LMAX, long_len)
    result = jnp.where(jnp.arange(DOCS)[None, :] == chosen[:, None], long_len[:, None], short)
    return result.reshape(-1).astype(jnp.int32)


def draw_memory_lengths(key, part):
    key = jax.random.fold_in(key, 14)
    shards = DOCS_ALL // DOCS
    base_key, place_key = jax.random.split(key)
    result = jax.random.randint(base_key, (shards * DOCS,), 1, ELEN + 1)
    place = jax.random.randint(place_key, (), 0, shards * DOCS)
    result = jnp.where(jnp.arange(shards * DOCS) == place, ELEN, result)
    return result.astype(jnp.int32)


def level_of(stream_key, dims, cuts, smallest, largest):
    loudness, own = 1.0, jax.random.fold_in(stream_key, 6)
    for dim, blocks in cuts:
        steps = jnp.exp(jax.random.uniform(jax.random.fold_in(own, dim), (blocks,), jnp.float32, smallest / len(cuts), largest / len(cuts)))
        loudness = loudness * jnp.repeat(steps, dims[dim] // blocks).reshape([-1 if axis == dim else 1 for axis in range(len(dims))])
    return loudness


def normal_values(own_key, extent, scale, bound, cuts=(), kind=jnp.bfloat16):
    level = level_of(own_key, extent, cuts, -0.22, 0.18) if cuts else 1.0
    array = jax.random.normal(own_key, extent, jnp.float32) * scale * level
    return jnp.minimum(jnp.maximum(array, -bound), bound).astype(kind)


def setup_inputs(seed: int = 0) -> dict:
    seeds = jax.random.split(jax.random.key(seed), 27)
    tokens = normal_values(seeds[0], (TOKENS, D), 1.0, 6.0, ((0, 32),))
    memory = normal_values(seeds[1], (TOKENS, D), 1.0, 6.0, ((0, 32),))
    cotangent = draw_cotangent(jax.random.fold_in(seeds[26], 71), 0)
    lengths = draw_lengths(jax.random.fold_in(seeds[26], 71), 0)
    memory_lengths = draw_memory_lengths(jax.random.fold_in(seeds[26], 71), 0)
    self_weight = normal_values(seeds[5], (3, D, D), D ** -0.5, 0.21875, ((1, 32), (2, 4)), jnp.float32)
    self_moment = normal_values(seeds[6], (3, D, D), (0.11 * PARAMS ** -0.5), 0.00021362305, ((1, 32), (2, 4)), jnp.float32)
    self_square = jnp.clip(jnp.exp(math.log(4.237345474500387e-10) - 1.3862944 * jax.random.uniform(seeds[7], (3, D, D), jnp.float32) ** level_of(seeds[7], (3, D, D), ((1, 32), (2, 4)), -0.2, 0.2)), 1.0593363686250967e-10, 4.237345474500387e-10)
    cross_weight = normal_values(seeds[8], (3, D, D), D ** -0.5, 0.21875, ((1, 32), (2, 4)), jnp.float32)
    cross_moment = normal_values(seeds[9], (3, D, D), (0.11 * PARAMS ** -0.5), 0.00021362305, ((1, 32), (2, 4)), jnp.float32)
    cross_square = jnp.clip(jnp.exp(math.log(4.237345474500387e-10) - 1.3862944 * jax.random.uniform(seeds[10], (3, D, D), jnp.float32) ** level_of(seeds[10], (3, D, D), ((1, 32), (2, 4)), -0.2, 0.2)), 1.0593363686250967e-10, 4.237345474500387e-10)
    merge_weight = normal_values(seeds[11], (2, D, D), (D // 8) ** -0.5, 0.625, ((1, 4), (2, 32)), jnp.float32)
    merge_moment = normal_values(seeds[12], (2, D, D), (0.11 * PARAMS ** -0.5), 0.00021362305, ((1, 4), (2, 32)), jnp.float32)
    merge_square = jnp.clip(jnp.exp(math.log(4.237345474500387e-10) - 1.3862944 * jax.random.uniform(seeds[13], (2, D, D), jnp.float32) ** level_of(seeds[13], (2, D, D), ((1, 4), (2, 32)), -0.2, 0.2)), 1.0593363686250967e-10, 4.237345474500387e-10)
    expand_weight = normal_values(seeds[14], (D, FF), D ** -0.5, 0.21875, ((0, 32), (1, 4)), jnp.float32)
    expand_moment = normal_values(seeds[15], (D, FF), (0.11 * PARAMS ** -0.5), 0.00021362305, ((0, 32), (1, 4)), jnp.float32)
    expand_square = jnp.clip(jnp.exp(math.log(4.237345474500387e-10) - 1.3862944 * jax.random.uniform(seeds[16], (D, FF), jnp.float32) ** level_of(seeds[16], (D, FF), ((0, 32), (1, 4)), -0.2, 0.2)), 1.0593363686250967e-10, 4.237345474500387e-10)
    shrink_weight = normal_values(seeds[17], (FF, D), FF ** -0.5, 0.109375, ((0, 4), (1, 32)), jnp.float32)
    shrink_moment = normal_values(seeds[18], (FF, D), (0.11 * PARAMS ** -0.5), 0.00021362305, ((0, 4), (1, 32)), jnp.float32)
    shrink_square = jnp.clip(jnp.exp(math.log(4.237345474500387e-10) - 1.3862944 * jax.random.uniform(seeds[19], (FF, D), jnp.float32) ** level_of(seeds[19], (FF, D), ((0, 4), (1, 32)), -0.2, 0.2)), 1.0593363686250967e-10, 4.237345474500387e-10)
    norm_gains = draw_norm_gains(jax.random.fold_in(seeds[26], 71), 0)
    gains_moment = normal_values(seeds[21], (3, D), (0.6 * PARAMS ** -0.5), 0.0012207031, ((1, 32),), jnp.float32)
    gains_square = jnp.clip(jnp.exp(math.log(1.2712036756568068e-08) - 1.3862944 * jax.random.uniform(seeds[22], (3, D), jnp.float32) ** level_of(seeds[22], (3, D), ((1, 32),), -0.2, 0.2)), 3.178009189142017e-09, 1.2712036756568068e-08)
    bucket_bias = normal_values(seeds[23], (H, NB), 1.0, 4.0, ((0, 4), (1, 32)), jnp.float32)
    bias_moment = normal_values(seeds[24], (H, NB), (0.6 * PARAMS ** -0.5), 0.0012207031, ((0, 4), (1, 32)), jnp.float32)
    bias_square = jnp.clip(jnp.exp(math.log(1.2712036756568068e-08) - 1.3862944 * jax.random.uniform(seeds[25], (H, NB), jnp.float32) ** level_of(seeds[25], (H, NB), ((0, 4), (1, 32)), -0.2, 0.2)), 3.178009189142017e-09, 1.2712036756568068e-08)
    return {"tokens": tokens, "memory": memory, "cotangent": cotangent, "lengths": lengths, "memory_lengths": memory_lengths, "self_weight": self_weight, "self_moment": self_moment, "self_square": self_square, "cross_weight": cross_weight, "cross_moment": cross_moment, "cross_square": cross_square, "merge_weight": merge_weight, "merge_moment": merge_moment, "merge_square": merge_square, "expand_weight": expand_weight, "expand_moment": expand_moment, "expand_square": expand_square, "shrink_weight": shrink_weight, "shrink_moment": shrink_moment, "shrink_square": shrink_square, "norm_gains": norm_gains, "gains_moment": gains_moment, "gains_square": gains_square, "bucket_bias": bucket_bias, "bias_moment": bias_moment, "bias_square": bias_square}


bucket_edges = (19, 21, 24, 27, 31, 35, 40, 46, 52, 59, 67, 77, 87, 99, 113)
epsilon = 1e-06
negative = -1e+30
beta_one = 0.9
beta_two = 0.999
adam_epsilon = 1e-08
clip_norm = 1.0
rate_matrix = 0.03
rate_small = 1.0
decay_matrix = 0.01

@jax.custom_vjp
def low(v):
    return lax.optimization_barrier(v.astype(jnp.bfloat16)).astype(jnp.float32)

@jax.custom_vjp
def low_back(v):
    return v

def low_keep(v):
    return (low(v), None)

def low_pass(kept, grad):
    return (grad,)

def back_keep(v):
    return (v, None)

def back_low(kept, grad):
    return (low(grad),)
low.defvjp(low_keep, low_pass)
low_back.defvjp(back_keep, back_low)

def rounded(value):
    return low_back(low(value))

def matmul(left_side, right_side):
    return jnp.dot(left_side, right_side, precision=lax.Precision.HIGHEST)

def normed(value, gain_row):
    return value * lax.rsqrt(lax.optimization_barrier(jnp.mean(value * value, axis=-1, keepdims=True)) + epsilon) * gain_row

def layout(sizes_row, row_count):
    end_rows = jnp.cumsum(sizes_row).astype(jnp.int32)
    row_index = jnp.arange(row_count, dtype=jnp.int32)
    passed = row_index[:, None] >= end_rows[None, :]
    doc_ids = lax.optimization_barrier(jnp.sum(passed.astype(jnp.int32), axis=1)).astype(jnp.int32)
    start_rows = lax.optimization_barrier(jnp.sum(jnp.where(passed, sizes_row[None, :], 0), axis=1)).astype(jnp.int32)
    return (doc_ids, row_index - start_rows, doc_ids < sizes_row.shape[0])

def bucket_of(distance):
    bucket = jnp.minimum(distance, 16).astype(jnp.int32)
    for edge_value in bucket_edges:
        bucket = bucket + (distance >= edge_value).astype(jnp.int32)
    return bucket

def split_heads(matrix):
    return matrix.reshape(matrix.shape[0], -1, HD)

def attention(queries, key_rows, value_rows, allowed, bias_block):
    raw_scores = low_back(jnp.einsum('qhd,khd->hqk', split_heads(queries), split_heads(key_rows), precision=lax.Precision.HIGHEST))
    scores = jnp.where(allowed[None], raw_scores * HD ** (-0.5) + bias_block, negative)
    row_max = lax.optimization_barrier(jnp.max(scores, axis=-1, keepdims=True))
    exponent = jnp.exp(scores - row_max)
    weights_block = low(exponent / lax.optimization_barrier(jnp.sum(exponent, axis=-1, keepdims=True)))
    mixed_block = jnp.einsum('hqk,khd->qhd', weights_block, split_heads(value_rows), precision=lax.Precision.HIGHEST)
    return rounded(mixed_block.reshape(queries.shape[0], -1))

def shard_layer(weights, token_rows, memory_rows, sizes_row, memory_sizes):
    self_weight, cross_weight, merge_weight, expand_weight, shrink_weight, norm_gains, bucket_bias = weights
    doc_ids, positions, present = layout(sizes_row, TOK)
    memory_ids, _, memory_present = layout(memory_sizes, TOK)
    first_in = low(normed(token_rows, norm_gains[0]))
    queries = rounded(matmul(first_in, self_weight[0]))
    key_rows = rounded(matmul(first_in, self_weight[1]))
    value_rows = rounded(matmul(first_in, self_weight[2]))
    distance = jnp.maximum(positions[:, None] - positions[None, :], 0)
    bias_block = jnp.take(bucket_bias, bucket_of(distance), axis=1)
    causal = (doc_ids[:, None] == doc_ids[None, :]) & (positions[:, None] >= positions[None, :])
    self_mixed = attention(queries, key_rows, value_rows, causal, bias_block)
    after_self = token_rows + low_back(matmul(self_mixed, merge_weight[0]))
    second_in = low(normed(after_self, norm_gains[1]))
    cross_queries = rounded(matmul(second_in, cross_weight[0]))
    cross_keys = rounded(matmul(memory_rows, cross_weight[1]))
    cross_values = rounded(matmul(memory_rows, cross_weight[2]))
    linked = (doc_ids[:, None] == memory_ids[None, :]) & memory_present[None, :]
    cross_mixed = attention(cross_queries, cross_keys, cross_values, linked, 0.0)
    after_cross = after_self + low_back(matmul(cross_mixed, merge_weight[1]))
    third_in = low(normed(after_cross, norm_gains[2]))
    hidden = low_back(matmul(third_in, expand_weight))
    activated = low(jax.nn.gelu(hidden, approximate=False))
    result = after_cross + low_back(matmul(activated, shrink_weight))
    return result * present[:, None].astype(jnp.float32)

def forward(masters, token_all, memory_all, sizes_all, memory_sizes_all):
    weights = tuple((low(master) for master in masters))

    def single(pieces):
        return shard_layer(weights, pieces[0], pieces[1], pieces[2], pieces[3])
    checked = jax.checkpoint(single)
    pieces = (token_all.reshape(N_WIDE, TOK, D), memory_all.reshape(N_WIDE, TOK, D), sizes_all.reshape(N_WIDE, DOCS), memory_sizes_all.reshape(N_WIDE, DOCS))
    results = lax.map(checked, pieces)
    return results.reshape(N_WIDE * TOK, D)

def adamw(weight, moment, square, gradient, factor, rate, decay):
    clipped = gradient * factor
    moment_new = beta_one * moment + (1.0 - beta_one) * clipped
    square_new = beta_two * square + (1.0 - beta_two) * clipped * clipped
    corrected = moment_new / (1.0 - beta_one ** STEP)
    scaled = square_new / (1.0 - beta_two ** STEP)
    weight_new = weight - rate * (corrected / (jnp.sqrt(scaled) + adam_epsilon) + decay * weight)
    return (weight_new, moment_new, square_new)

def reference(tokens, memory, cotangent, lengths, memory_lengths, self_weight, self_moment, self_square, cross_weight, cross_moment, cross_square, merge_weight, merge_moment, merge_square, expand_weight, expand_moment, expand_square, shrink_weight, shrink_moment, shrink_square, norm_gains, gains_moment, gains_square, bucket_bias, bias_moment, bias_square):
    masters = (self_weight, cross_weight, merge_weight, expand_weight, shrink_weight, norm_gains, bucket_bias)
    moments = (self_moment, cross_moment, merge_moment, expand_moment, shrink_moment, gains_moment, bias_moment)
    squares = (self_square, cross_square, merge_square, expand_square, shrink_square, gains_square, bias_square)

    def whole(master_tuple, token_all, memory_all):
        return forward(master_tuple, token_all, memory_all, lengths, memory_lengths)
    layer, pullback = jax.vjp(whole, masters, tokens.astype(jnp.float32), memory.astype(jnp.float32))
    weight_grads, tokens_gradient, memory_gradient = pullback(cotangent.astype(jnp.float32))
    total = jnp.zeros((), jnp.float32)
    for piece_grad in weight_grads:
        total = total + jnp.sum(piece_grad * piece_grad)
    gradient_norm = jnp.sqrt(total)
    factor = clip_norm / jnp.maximum(gradient_norm, clip_norm)
    rates = (rate_matrix,) * 5 + (rate_small,) * 2
    decays = (decay_matrix,) * 5 + (0.0,) * 2
    updated = [adamw(masters[index], moments[index], squares[index], weight_grads[index], factor, rates[index], decays[index]) for index in range(7)]
    return (layer.astype(jnp.bfloat16), tokens_gradient, memory_gradient, gradient_norm, updated[0][0], updated[0][1], updated[0][2], updated[1][0], updated[1][1], updated[1][2], updated[2][0], updated[2][1], updated[2][2], updated[3][0], updated[3][1], updated[3][2], updated[4][0], updated[4][1], updated[4][2], updated[5][0], updated[5][1], updated[5][2], updated[6][0], updated[6][1], updated[6][2])
```

```python
import math
import types

import jax
import jax.numpy as jnp
from jax import lax
from jax.experimental import pallas as pl
from jax.experimental.pallas import tpu as pltpu
from jax.sharding import PartitionSpec as P

F32 = jnp.float32
BF16 = jnp.bfloat16
MESH = pl.DeviceIdType.MESH
STEP = 10
bucket_edges = (19, 21, 24, 27, 31, 35, 40, 46, 52, 59, 67, 77, 87, 99, 113)
epsilon = 1e-06
negative = -1e30
beta_one = 0.9
beta_two = 0.999
adam_epsilon = 1e-08
clip_norm = 1.0
rate_matrix = 0.03
rate_small = 1.0
decay_matrix = 0.01
SCALE = 0.125
COPIES = 384

weight_names = [part + kind for part in "scmehgb" for kind in "wms"]
input_names = ["tokens", "memory", "cot", "lens", "mlens"] + weight_names
output_names = ["lo", "tg", "mg", "norm"] + [name + "n" for name in weight_names]
step_inputs = ["tokens", "memory", "cot", "lens", "mlens"] + [part + "w" for part in "scmehgb"]
step_outputs = ["lo", "tg", "mg", "grads", "small", "norm"]

scratch_shapes = dict(
    pk=((2, 24, 2112), F32),
    cat=((2, 24, 2112), F32),
    ZS=((4, 48, 576), BF16),
    W=((7, 16, 48, 768), BF16),
    GN=((8, 768), F32),
    GS=((8, 768), F32),
    DC=((512, 128), jnp.int32),
    DR=((8, 512), jnp.int32),
    MR=((8, 512), jnp.int32),
    TOK=((512, 768), BF16),
    MEM=((512, 768), BF16),
    FG=((512, 768), BF16),
    FI=((512, 768), BF16),
    SI=((512, 768), BF16),
    TI=((512, 768), BF16),
    COG=((512, 768), BF16),
    LO=((512, 768), BF16),
    TG=((512, 768), BF16),
    MG=((512, 768), BF16),
    QH=((3, 512, 64), BF16),
    KH=((3, 512, 64), BF16),
    VH=((3, 512, 64), BF16),
    CQH=((3, 512, 64), BF16),
    CKH=((3, 512, 64), BF16),
    CVH=((3, 512, 64), BF16),
    DMH=((3, 512, 64), BF16),
    CDMH=((3, 512, 64), BF16),
    SM=((512, 192), BF16),
    CM=((512, 192), BF16),
    M0=((768, 192), BF16),
    M1=((768, 192), BF16),
    SMF=((4, 4, 64, 384), BF16),
    CMF=((4, 4, 64, 384), BF16),
    DQF=((4, 4, 64, 384), BF16),
    T=((3, 2, 128, 128), F32),
    BK=((2, 128, 128), jnp.int32),
    PS=((3, 4, 128, 384), F32),
    PC=((3, 512, 512), F32),
    RS=((3, 4, 128, 384), BF16),
    RC=((3, 512, 512), BF16),
    AGR=((512, 768), F32),
    ACT=((512, 768), BF16),
    HG=((512, 768), BF16),
    DCQ=((512, 192), BF16),
    DCKV=((512, 384), BF16),
    DQKV=((512, 576), BF16),
    AS=((512, 768), F32),
    AC=((128, 768), F32),
    CT=((128, 768), F32),
    ST=((128, 768), F32),
    AB=((3, 3, 128, 128), F32),
    BR=((96, 128), F32),
    zsend=((2, 3, 128, 768), BF16),
    zrelay=((4, 2, 64, 768), BF16),
    zrecv=((4, 2, 128, 768), BF16),
    zown=((2, 128, 768), F32),
    ztmp=((2, 2, 64, 768), F32),
    GB=((2, 16, 48, 768), BF16),
    RB=((4, 16, 48, 384), BF16),
    HF=((2, 16, 48, 384), F32),
    HB=((2, 16, 48, 384), BF16),
    RL=((4, 4, 48, 384), BF16),
    FB=((4, 4, 48, 384), BF16),
    RV=((4, 2, 4, 48, 384), BF16),
    CB=((4, 4, 48, 384), BF16),
    RCV=((4, 4, 48, 384), BF16),
    FN=((4, 2, 24, 384), F32),
    RG=((4, 2, 24, 384), F32),
    EX=((5, 4, 16, 768), F32),
    SC=((5, 4, 8, 128), F32),
)
semaphore_shapes = dict(ssem=COPIES, rsem=COPIES, lsem=8)


def dot(a, b):
    return jnp.dot(a, b, preferred_element_type=F32)


def dot_nt(a, b):
    return lax.dot_general(a, b, (((1,), (1,)), ((), ())), preferred_element_type=F32)


def dot_tn(a, b):
    return lax.dot_general(a, b, (((0,), (0,)), ((), ())), preferred_element_type=F32)


def mod4(v):
    return lax.rem(v + 4, 4)


def mult(v, n):
    return pl.multiple_of(v, n)


def norm_parts(value):
    scale = lax.rsqrt(jnp.mean(value * value, axis=-1, keepdims=True) + epsilon)
    return scale, value * scale


def norm_back(value, gain_row, grad):
    scale, unit = norm_parts(value)
    gain_grad = jnp.sum(grad * unit, axis=0, keepdims=True)
    inner = grad * gain_row
    value_grad = scale * (inner - unit * jnp.mean(inner * unit, axis=-1, keepdims=True))
    return value_grad, gain_grad


def softmax(scores):
    top = jnp.max(scores, axis=-1, keepdims=True)
    exponent = jnp.exp(scores - top)
    return exponent * (1.0 / jnp.sum(exponent, axis=-1, keepdims=True))


def adamw(weight, moment, square, gradient, factor, rate, decay):
    clipped = gradient * factor
    moment_new = beta_one * moment + (1.0 - beta_one) * clipped
    square_new = beta_two * square + (1.0 - beta_two) * clipped * clipped
    corrected = moment_new / (1.0 - beta_one**STEP)
    scaled = square_new / (1.0 - beta_two**STEP)
    weight_new = weight - rate * (corrected / (jnp.sqrt(scaled) + adam_epsilon) + decay * weight)
    return (weight_new, moment_new, square_new)


def kernel(*refs):
    names = step_inputs + step_outputs + list(scratch_shapes) + list(semaphore_shapes)
    s = types.SimpleNamespace(**dict(zip(names, refs)))
    w = lax.axis_index("wide")
    z = lax.axis_index("narrow")
    c = lax.rem(w, 2)
    y = lax.rem(lax.div(w, 2), 4)
    x = lax.div(w, 8)
    other = w + 1 - 2 * c
    zl, zr, zf = mod4(z - 1), mod4(z + 1), mod4(z + 2)
    p1 = x * (1 - c) + y * c
    p2 = y * (1 - c) + x * c
    s1, s2 = 4 - 3 * c, 1 + 3 * c

    def chip(a, b):
        return s1 * a + s2 * b

    def dev(a, b):
        return 2 * chip(a, b) + c

    def wide_at(xx, yy):
        return (xx * 4 + yy) * 2 + c

    started = []
    pending = {}
    local = []

    def move(src, dst):
        op = pltpu.make_async_copy(src, dst, s.lsem.at[len(local)])
        op.start()
        local.append(op)
        return op

    def settle(ops):
        for op in ops:
            op.wait_send()
            del pending[id(op)]

    def send(src, dst, to_w=None, to_z=None):
        slot = len(started)
        assert slot < COPIES
        op = pltpu.make_async_remote_copy(
            src_ref=src,
            dst_ref=dst,
            send_sem=s.ssem.at[slot],
            recv_sem=s.rsem.at[slot],
            device_id=(w if to_w is None else to_w, z if to_z is None else to_z),
            device_id_type=MESH,
        )
        op.start()
        started.append(op)
        pending[id(op)] = op
        return op

    barrier = pltpu.get_barrier_semaphore()
    peers = [(other, z)]
    for d in (1, 2, 3):
        peers += [(wide_at(mod4(x + d), y), z), (wide_at(x, mod4(y + d)), z), (w, mod4(z + d))]
    for peer in peers:
        pl.semaphore_signal(barrier, inc=1, device_id=peer, device_id_type=MESH)

    loads = [move(s.tokens, s.TOK), move(s.cot, s.FG), move(s.memory, s.MEM)]

    lane = lax.broadcasted_iota(jnp.int32, (24, 128), 1)
    row24 = lax.broadcasted_iota(jnp.int32, (24, 128), 0)
    pick = lax.broadcasted_iota(jnp.int32, (24, 24), 0) == lax.broadcasted_iota(
        jnp.int32, (24, 24), 1
    )
    extra = jnp.zeros((24, 128), F32)
    for k in range(3):
        gain = s.gw[k : k + 1, :]
        column = jnp.sum(jnp.where(pick, gain, 0.0), axis=1, keepdims=True)
        extra = jnp.where(lane == k, column, extra)
        extra = jnp.where((lane == 3 + k) & (row24 == 0), s.bw[0:1, k : k + 1], extra)
    for h in range(2):
        s.pk[h, :, 768:1152] = s.ew[:, 384 * h : 384 * h + 384]
        s.pk[h, :, 1152:1536] = s.hw[:, 384 * h : 384 * h + 384]
        s.pk[h, :, 1536:2112] = jnp.concatenate([s.mw[0], s.mw[1], s.cw[0]], axis=1)
    s.pk[0, :, 0:384] = jnp.concatenate([s.sw[0], s.sw[1]], axis=1)
    s.pk[1, :, 0:384] = jnp.concatenate([s.sw[2], extra, jnp.zeros((24, 64), F32)], axis=1)
    s.pk[0, :, 384:768] = jnp.concatenate([s.cw[1], s.cw[2]], axis=1)
    s.pk[1, :, 384:768] = jnp.concatenate([s.cw[0], jnp.zeros((24, 192), F32)], axis=1)

    pl.semaphore_wait(barrier, len(peers))
    pair = send(s.pk.at[1 - c], s.cat.at[c], to_w=other)
    s.cat[c] = s.pk[c]

    row_col = lax.broadcasted_iota(jnp.int32, (512, 128), 0)
    row_row = lax.broadcasted_iota(jnp.int32, (8, 512), 1)
    doc_col = jnp.zeros((512, 128), jnp.int32)
    doc_row = jnp.zeros((8, 512), jnp.int32)
    mem_row = jnp.zeros((8, 512), jnp.int32)
    end, mem_end = jnp.int32(0), jnp.int32(0)
    for k in range(8):
        end = end + s.lens[k]
        mem_end = mem_end + s.mlens[k]
        doc_col = doc_col + (row_col >= end).astype(jnp.int32)
        doc_row = doc_row + (row_row >= end).astype(jnp.int32)
        mem_row = mem_row + (row_row >= mem_end).astype(jnp.int32)
    s.DC[...] = doc_col
    s.DR[...] = doc_row
    s.MR[...] = jnp.where(mem_row < 8, mem_row, -1)
    pair.wait_recv()
    block = s.cat[...].reshape(48, 2112).astype(BF16)
    me = chip(p1, p2)
    c384 = mult(384 * c, 128)
    o384 = mult(384 * (1 - c), 128)
    for g in range(4):
        s.W[g, me, :, pl.ds(c384, 384)] = block[:, 384 * g : 384 * g + 384]

    def block_at(g, index):
        return s.W.at[g, index, :, pl.ds(c384, 384)]

    class Gather:
        def __init__(self, g, eager=False):
            self.g, self.eager, self.four = g, eager, []
            ref = block_at(g, me)
            self.one = {d: send(ref, ref, to_w=dev(mod4(p1 + d), p2)) for d in (1, 3, 2)}

        def share(self, ref):
            self.four.append(send(ref, ref, to_w=other))

        def second(self):
            self.two = {}
            for r, d in ((0, None), (3, 1), (1, 3), (2, 2)):
                if d is not None:
                    self.one[d].wait_recv()
                ref = block_at(self.g, chip(mod4(p1 + r), p2))
                for way in (1, -1):
                    self.two[way, r] = send(ref, ref, to_w=dev(p1, mod4(p2 + way)))
                if self.eager:
                    self.share(ref)

        def third(self):
            self.three = []
            for r, way in ((0, 1), (2, -1), (1, 1), (3, -1)):
                self.two[way, r].wait_recv()
                ref = block_at(self.g, chip(mod4(p1 + r), mod4(p2 - way)))
                self.three.append((r, send(ref, ref, to_w=dev(p1, mod4(p2 + way)))))
                if self.eager:
                    self.share(ref)

        def fourth(self):
            for r, way in ((2, 1), (0, -1), (3, 1), (1, -1)):
                self.two[way, r].wait_recv()
                if self.eager:
                    self.share(block_at(self.g, chip(mod4(p1 + r), mod4(p2 - way))))
            for r, op in self.three:
                op.wait_recv()
                if self.eager:
                    self.share(block_at(self.g, chip(mod4(p1 + r), mod4(p2 + 2))))
            if not self.eager:
                self.share(s.W.at[self.g, :, :, pl.ds(c384, 384)])

        def done(self):
            for op in self.four:
                op.wait_recv()

    gather = {0: Gather(0, True)}
    s.ZS[z] = block[:, 1536:2112]
    stage = [send(s.ZS.at[z], s.ZS.at[z], to_z=to) for to in (zr, zl, zf)]
    for g in (1, 3, 2):
        gather[g] = Gather(g)
    gather[0].second()
    for op in stage:
        op.wait_recv()
    for k, g in enumerate((4, 5, 6)):
        piece = slice(192 * k, 192 * k + 192)
        two_parts = [s.ZS[2 * c, :, piece], s.ZS[2 * c + 1, :, piece]]
        s.W[g, me, :, pl.ds(c384, 384)] = jnp.concatenate(two_parts, axis=1)
        if g != 6:
            gather[g] = Gather(g)
    gather[0].third()
    gather[4].second()
    gather[0].fourth()
    gather[1].second()
    gather[6] = Gather(6)
    loads[1].wait()
    for t in range(4):
        rows = pl.ds(128 * t, 128)
        seed = jnp.where(s.DC[rows, 0:1] < 8, s.FG[rows, :].astype(F32), 0.0)
        s.FG[rows, :] = seed.astype(BF16)
    loads[0].wait()
    loads[2].wait()

    tile_row = lax.broadcasted_iota(jnp.int32, (128, 128), 0)
    tile_col = lax.broadcasted_iota(jnp.int32, (128, 128), 1)
    for delta in range(2):
        distance = jnp.maximum(128 * delta + tile_row - tile_col, 0)
        bucket = jnp.minimum(distance, 16)
        for edge in bucket_edges:
            bucket = bucket + (distance >= edge).astype(jnp.int32)
        s.BK[delta] = bucket

    gather[0].done()

    eye = (
        lax.broadcasted_iota(jnp.int32, (8, 256), 0) + 64
        == lax.broadcasted_iota(jnp.int32, (8, 256), 1)
    ).astype(BF16)
    gains = dot_nt(eye, s.W[0, :, :, 512:768].reshape(768, 256))
    s.GN[...] = gains
    last_bias = []
    for h in range(3):
        entry = [gains[3 + h : 4 + h, 24 * k : 24 * k + 1] for k in range(32)]
        last_bias.append(entry[31])
        for delta in range(2):
            bucket = s.BK[delta]
            tile = jnp.broadcast_to(entry[0], (128, 128))
            for k in range(1, 32):
                tile = jnp.where(bucket >= k, entry[k], tile)
            s.T[h, delta] = tile

    for t in range(4):
        rows = pl.ds(128 * t, 128)
        _, unit = norm_parts(s.TOK[rows, :].astype(F32))
        s.FI[rows, :] = (unit * gains[0:1]).astype(BF16)

    def weight(g, start, stop):
        return s.W[g, :, :, start:stop].reshape(768, stop - start)

    query_key = dot(s.FI[...], weight(0, 0, 384))
    for h in range(3):
        s.QH[h] = query_key[:, 64 * h : 64 * h + 64].astype(BF16)
        s.KH[h] = query_key[:, 192 + 64 * h : 256 + 64 * h].astype(BF16)
    value_rows = dot(s.FI[...], weight(0, 384, 576))
    for h in range(3):
        s.VH[h] = value_rows[:, 64 * h : 64 * h + 64].astype(BF16)
    gather[4].third()

    def band(i):
        low = max(0, i - 2)
        return slice(128 * low, 128 * (i + 1)), i - low + 1

    class TileSpread:
        def __init__(self, buffer, index):
            self.buffer, self.index = buffer, index
            self.near, self.far = {}, {}

        def send(self, k, value):
            tile = self.index(z, k)
            packed = jnp.concatenate([value[0:64], value[64:128]], axis=1)
            self.buffer[z, tile] = packed
            ref = self.buffer.at[z, tile]
            self.near[k] = (send(ref, ref, to_z=zr), send(ref, ref, to_z=zl))

        def relay(self, k):
            from_l, from_r = self.near[k]
            from_l.wait_recv()
            ref = self.buffer.at[zl, self.index(zl, k), pl.ds(0, 32)]
            far_l = send(ref, ref, to_z=zr)
            from_r.wait_recv()
            ref = self.buffer.at[zr, self.index(zr, k), pl.ds(32, 32)]
            self.far[k] = (far_l, send(ref, ref, to_z=zl))

        def done(self, k):
            for op in self.far[k]:
                op.wait_recv()

        def rows(self, tile):
            parts = [self.buffer[k, tile] for k in range(4)]
            top = jnp.concatenate([part[:, 0:192] for part in parts], axis=1)
            bottom = jnp.concatenate([part[:, 192:384] for part in parts], axis=1)
            return jnp.concatenate([top, bottom], axis=0)

    self_spread = TileSpread(s.SMF, lambda zz, k: k)
    for i in range(4):
        rows = slice(128 * i, 128 * i + 128)
        keys, count = band(i)
        width = 128 * count
        ahead = lax.broadcasted_iota(jnp.int32, (128, width), 0) - lax.broadcasted_iota(
            jnp.int32, (128, width), 1
        )
        allowed = (s.DC[rows, 0:1] == s.DR[0:1, keys]) & (ahead + 128 * (count - 1) >= 0)
        mixed = []
        for h in range(3):
            tiles = [jnp.broadcast_to(last_bias[h], (128, 128)), s.T[h, 1], s.T[h, 0]][-count:]
            bias = tiles[0] if count == 1 else jnp.concatenate(tiles, axis=1)
            raw = dot_nt(s.QH[h, rows, :], s.KH[h, keys, :])
            probs = softmax(jnp.where(allowed, raw * SCALE + bias, negative))
            s.PS[h, i, :, 0:width] = probs
            mixed.append(dot(probs.astype(BF16), s.VH[h, keys, :]))
        merged = jnp.concatenate(mixed, axis=1).astype(BF16)
        s.SM[rows, :] = merged
        self_spread.send(i, merged)
        if i == 0:
            gather[1].third()
            gather[4].fourth()
        if i == 1:
            gather[5].second()
            self_spread.relay(0)
        if i == 2:
            gather[3].second()
            gather[1].fourth()
            self_spread.relay(1)

    def at(d):
        return pl.ds(mult(128 * d, 128), 128)

    class Scatter:
        made = []

        def __init__(self, part, order="zrlo"):
            n = self.n = len(Scatter.made)
            Scatter.made.append(self)
            if n >= 2:
                old = Scatter.made[n - 2]
                settle([old.relay_l, old.relay_r, old.right_a, old.right_b, old.left_a, old.left_b])

            def far():
                s.zsend[n % 2, 0] = part(zf).astype(BF16)
                self.relay_l = send(s.zsend.at[n % 2, 0, pl.ds(0, 64)], s.zrelay.at[n, 0], to_z=zr)
                self.relay_r = send(s.zsend.at[n % 2, 0, pl.ds(64, 64)], s.zrelay.at[n, 1], to_z=zl)

            def right():
                value = part(zr)
                s.ztmp[n % 2, 0] = value[0:64]
                s.zsend[n % 2, 1, 64:128] = value[64:128].astype(BF16)
                self.right_b = send(
                    s.zsend.at[n % 2, 1, pl.ds(64, 64)], s.zrecv.at[n, 0, pl.ds(64, 64)], to_z=zr
                )

            def left():
                value = part(zl)
                s.ztmp[n % 2, 1] = value[64:128]
                s.zsend[n % 2, 2, 0:64] = value[0:64].astype(BF16)
                self.left_a = send(
                    s.zsend.at[n % 2, 2, pl.ds(0, 64)], s.zrecv.at[n, 1, pl.ds(0, 64)], to_z=zl
                )

            def own():
                s.zown[n % 2] = part(z)

            for step in order:
                {"z": far, "r": right, "l": left, "o": own}[step]()

        def middle(self):
            n = self.n
            self.relay_l.wait_recv()
            s.zsend[n % 2, 1, 0:64] = (s.ztmp[n % 2, 0] + s.zrelay[n, 0].astype(F32)).astype(BF16)
            self.right_a = send(
                s.zsend.at[n % 2, 1, pl.ds(0, 64)], s.zrecv.at[n, 0, pl.ds(0, 64)], to_z=zr
            )
            self.relay_r.wait_recv()
            s.zsend[n % 2, 2, 64:128] = (s.ztmp[n % 2, 1] + s.zrelay[n, 1].astype(F32)).astype(BF16)
            self.left_b = send(
                s.zsend.at[n % 2, 2, pl.ds(64, 64)], s.zrecv.at[n, 1, pl.ds(64, 64)], to_z=zl
            )

        def total(self):
            n = self.n
            for op in (self.right_b, self.left_a, self.right_a, self.left_b):
                op.wait_recv()
            return s.zown[n % 2] + s.zrecv[n, 0].astype(F32) + s.zrecv[n, 1].astype(F32)

    class Spread:
        def __init__(self, ref):
            self.ref = ref
            mine = ref.at[at(z)]
            self.from_l = send(mine, mine, to_z=zr)
            self.from_r = send(mine, mine, to_z=zl)

        def half(self, d, start):
            return self.ref.at[pl.ds(mult(128 * d + start, 64), 64)]

        def middle(self):
            self.from_l.wait_recv()
            ref = self.half(zl, 0)
            self.far_l = send(ref, ref, to_z=zr)
            self.from_r.wait_recv()
            ref = self.half(zr, 64)
            self.far_r = send(ref, ref, to_z=zl)

        def done(self):
            self.far_l.wait_recv()
            self.far_r.wait_recv()

    def own_heads(g):
        half = s.W[g, :, :, pl.ds(mult(384 * lax.div(z, 2), 128), 384)].reshape(768, 384)
        return jnp.where(lax.rem(z, 2) == 0, half[:, 0:192], half[:, 192:384])

    gather[1].done()
    keys_values = dot(s.MEM[...], weight(1, 0, 384))
    for h in range(3):
        s.CKH[h] = keys_values[:, 64 * h : 64 * h + 64].astype(BF16)
        s.CVH[h] = keys_values[:, 192 + 64 * h : 256 + 64 * h].astype(BF16)
    gather[4].done()
    self_spread.relay(2)
    gather[5].third()
    cross_spread = TileSpread(s.CMF, lambda zz, k: k)
    for i in range(4):
        rows = slice(128 * i, 128 * i + 128)
        self_spread.done(i)
        after_self = s.TOK[rows, :].astype(F32) + dot_nt(self_spread.rows(i), weight(4, 0, 768))
        s.AS[rows, :] = after_self
        second_in = (norm_parts(after_self)[1] * s.GN[1:2, :]).astype(BF16)
        s.SI[rows, :] = second_in
        queries = dot(second_in, weight(1, 384, 576)).astype(BF16)
        if i == 0:
            self_spread.relay(3)
            gather[5].fourth()
        allowed = s.DC[rows, 0:1] == s.MR[0:1, :]
        mixed = []
        for h in range(3):
            query = queries[:, 64 * h : 64 * h + 64]
            s.CQH[h, rows, :] = query
            raw = dot_nt(query, s.CKH[h])
            probs = softmax(jnp.where(allowed, raw * SCALE, negative))
            s.PC[h, rows, :] = probs
            mixed.append(dot(probs.astype(BF16), s.CVH[h]))
        merged = jnp.concatenate(mixed, axis=1).astype(BF16)
        s.CM[rows, :] = merged
        cross_spread.send(i, merged)
        if i == 0:
            gather[3].third()
            gather[2].second()
        if i == 1:
            cross_spread.relay(0)
            gather[3].fourth()
        if i == 2:
            cross_spread.relay(1)
            gather[2].third()
            gather[6].second()
    cross_spread.relay(2)
    gather[2].fourth()
    gather[3].done()
    for t in range(2):
        rows = slice(256 * t, 256 * t + 256)
        s.AGR[rows, :] = dot(s.FG[rows, :], weight(3, 0, 768))
    gather[5].done()
    cross_spread.relay(3)
    gather[6].third()

    def cross_merge(tile, rows):
        return s.AS[rows, :] + dot_nt(cross_spread.rows(tile), weight(5, 0, 768))

    for i in range(4):
        rows = slice(128 * i, 128 * i + 128)
        cross_spread.done(i)
        s.TI[rows, :] = (norm_parts(cross_merge(i, rows))[1] * s.GN[2:3, :]).astype(BF16)
    gather[2].done()
    gather[6].fourth()

    def feed_chunk(d):
        rows = at(d)
        hidden = dot(s.TI[rows, :], weight(2, 0, 768))
        phi = 0.5 + 0.5 * lax.erf(hidden * math.sqrt(0.5))
        slope = phi + hidden * jnp.exp(-0.5 * hidden * hidden) * (1.0 / math.sqrt(2.0 * math.pi))
        s.ACT[rows, :] = (hidden * phi).astype(BF16)
        hidden_grad = (s.AGR[rows, :] * slope).astype(BF16)
        s.HG[rows, :] = hidden_grad
        return dot_nt(hidden_grad, weight(2, 0, 768))

    third_sum = Scatter(feed_chunk)

    grad_place = {2: 0, 3: 1, 1: 0, 0: 1}
    held = {}

    def store_grad(g, half, pairs):
        place = grad_place[g]
        if place in held and held[place].g != g and id(held[place].pair) in pending:
            settle([held[place].pair])
        for k in range(2):
            columns = slice(384 * k, 384 * k + 384)
            values = [
                right[columns, :] if left is None else dot_tn(left[:, columns], right).astype(BF16)
                for left, right in pairs
            ]
            value = values[0] if len(values) == 1 else jnp.concatenate(values, axis=1)
            s.GB[place, 8 * k : 8 * k + 8, :, 384 * half : 384 * half + 384] = value.reshape(
                8, 48, 384
            )

    def block_sum(a, b):
        return a.astype(F32) + b.astype(F32)

    class Reduce:
        def __init__(self, g):
            self.g = g
            self.place = grad_place[g]
            self.total = s.HF.at[self.place]
            self.low = s.HB.at[self.place]
            self.pair = send(s.GB.at[self.place, :, :, pl.ds(o384, 384)], s.RB.at[g], to_w=other)

        def first(self):
            g = self.g
            self.pair.wait_recv()
            if self.place in held:
                old = held[self.place]
                settle(list(old.relay.values()) + list(old.direct.values()))
            held[self.place] = self
            total = block_sum(s.GB[self.place, :, :, pl.ds(c384, 384)], s.RB[g])
            self.total[...] = total
            self.low[...] = total.astype(BF16)
            self.relay, self.direct = {}, {}
            for r in range(4):
                way = 1 if r < 2 else -1
                self.relay[r] = send(
                    self.low.at[chip(mod4(p1 + r), mod4(p2 + 2))],
                    s.RL.at[g, r],
                    to_w=dev(p1, mod4(p2 + way)),
                )
            for r in range(4):
                way = -1 if r < 2 else 1
                self.direct[r] = send(
                    self.low.at[chip(mod4(p1 + r), mod4(p2 + way))],
                    s.RV.at[g, 0 if way == 1 else 1, r],
                    to_w=dev(p1, mod4(p2 + way)),
                )

        def second(self):
            g = self.g
            self.passed = {}
            for r in range(4):
                way = 1 if r < 2 else -1
                self.relay[r].wait_recv()
                total = self.total[chip(mod4(p1 + r), mod4(p2 + way))] + s.RL[g, r].astype(F32)
                s.FB[g, r] = total.astype(BF16)
                self.passed[r] = send(
                    s.FB.at[g, r], s.RV.at[g, 0 if way == 1 else 1, r], to_w=dev(p1, mod4(p2 + way))
                )

        def third(self):
            g = self.g
            self.last = {}
            for r in (1, 3, 2, 0):
                self.direct[r].wait_recv()
                self.passed[r].wait_recv()
                total = self.total[chip(mod4(p1 + r), p2)] + block_sum(s.RV[g, 0, r], s.RV[g, 1, r])
                if r:
                    s.CB[g, r] = total.astype(BF16)
                    self.last[r] = send(s.CB.at[g, r], s.RCV.at[g, r], to_w=dev(mod4(p1 + r), p2))
                else:
                    self.kept = total

        def fourth(self):
            g = self.g
            total = self.kept
            for r in (1, 3, 2):
                self.last[r].wait_recv()
                total = total + s.RCV[g, r].astype(F32)
            self.squares = jnp.sum(total * total, axis=0, keepdims=True)
            s.FN[g, 0] = total[0:24]
            s.FN[g, 1] = total[24:48]
            s.RG[g, c] = s.FN[g, c]
            self.give = send(s.FN.at[g, 1 - c], s.RG.at[g, c], to_w=other)

        def done(self):
            self.give.wait_recv()

    def two_halves(g, left, right):
        for half in range(2):
            store_grad(g, half, [(left, right[:, 384 * half : 384 * half + 384])])

    third_sum.middle()
    two_halves(2, s.TI, s.HG)
    expand_reduce = Reduce(2)
    after_cross = cross_merge(z, at(z))
    s.AC[...] = after_cross
    s.M1[...] = own_heads(5)
    two_halves(3, s.FG, s.ACT)
    shrink_reduce = Reduce(3)
    third_grad = third_sum.total()
    cross_path, third_gain = norm_back(s.AC[...], s.GN[2:3, :], third_grad)
    cross_total = s.FG[at(z), :].astype(F32) + cross_path
    s.CT[...] = cross_total
    s.COG[at(z), :] = cross_total.astype(BF16)
    spread = Spread(s.COG)
    expand_reduce.first()

    def turn_order(zz, k):
        return mod4(zz + (0, -1, 1, 2)[k])

    query_spread = TileSpread(s.DQF, turn_order)

    def cross_back(k):
        rows = at(turn_order(z, k))
        grad = dot(s.COG[rows, :], s.M1[...]).astype(BF16)
        parts = []
        for h in range(3):
            mixed_grad = grad[:, 64 * h : 64 * h + 64]
            s.CDMH[h, rows, :] = mixed_grad
            probs_grad = dot_nt(mixed_grad, s.CVH[h])
            probs = s.PC[h, rows, :]
            inner = jnp.sum(probs * probs_grad, axis=-1, keepdims=True)
            raw = (probs * (probs_grad - inner) * SCALE).astype(BF16)
            s.RC[h, rows, :] = raw
            parts.append(dot(raw, s.CKH[h]))
        merged = jnp.concatenate(parts, axis=1).astype(BF16)
        s.DCQ[rows, :] = merged
        query_spread.send(k, merged)

    cross_back(0)
    spread.middle()
    shrink_reduce.first()
    cross_back(1)
    query_spread.relay(0)
    cross_back(2)
    spread.done()
    query_spread.relay(1)
    cross_back(3)
    expand_reduce.second()
    query_spread.relay(2)
    parts = [dot_tn(s.RC[h], s.CQH[h]) for h in range(3)]
    parts += [dot_tn(s.PC[h].astype(BF16), s.CDMH[h]) for h in range(3)]
    s.DCKV[...] = jnp.concatenate(parts, axis=1).astype(BF16)
    query_spread.relay(3)
    feed_sum = Scatter(lambda d: dot_nt(s.ACT[at(d), :], weight(3, 0, 768)))
    shrink_reduce.second()
    expand_reduce.third()
    s.M0[...] = own_heads(4)
    store_grad(1, 0, [(s.MEM, s.DCKV[...])])
    store_grad(1, 1, [(s.SI, s.DCQ[...]), (s.COG, s.CM[...])])
    cross_reduce = Reduce(1)
    shrink_reduce.third()
    gather[6].done()
    for k in range(4):
        query_spread.done(k)

    s.SOG = s.TI
    for i in range(4):
        rows = slice(128 * i, 128 * i + 128)
        second_grad = dot_nt(query_spread.rows(i), weight(6, 0, 768))
        self_path, second_gain = norm_back(s.AS[rows, :], s.GN[1:2, :], second_grad)
        s.AS[rows, :] = self_path
        s.GS[i : i + 1, :] = second_gain
        self_out = (s.COG[rows, :].astype(F32) + self_path).astype(BF16)
        s.SOG[rows, :] = self_out
        keys, count = band(i)
        width = 128 * count
        grad = dot(self_out, s.M0[...]).astype(BF16)
        parts = []
        for h in range(3):
            mixed_grad = grad[:, 64 * h : 64 * h + 64]
            s.DMH[h, rows, :] = mixed_grad
            probs_grad = dot_nt(mixed_grad, s.VH[h, keys, :])
            probs = s.PS[h, i, :, 0:width]
            inner = jnp.sum(probs * probs_grad, axis=-1, keepdims=True)
            score_grad = probs * (probs_grad - inner)
            for t in range(count):
                delta = count - 1 - t
                tile = score_grad[:, 128 * t : 128 * t + 128]
                if i == delta:
                    s.AB[h, delta] = tile
                else:
                    s.AB[h, delta] += tile
            raw = (score_grad * SCALE).astype(BF16)
            s.RS[h, i, :, 0:width] = raw
            parts.append(dot(raw, s.KH[h, keys, :]))
        s.DQKV[rows, 0:192] = jnp.concatenate(parts, axis=1).astype(BF16)
        if i == 0:
            feed_sum.middle()
            cross_reduce.first()
            expand_reduce.fourth()
        if i == 1:
            layer_rows = s.AC[...] + feed_sum.total()
            layer_rows = jnp.where(s.DC[at(z), 0:1] < 8, layer_rows, 0.0)
            s.LO[at(z), :] = layer_rows.astype(BF16)
            layer_spread = Spread(s.LO)
            shrink_reduce.fourth()
        if i == 2:
            memory_sum = Scatter(lambda d: dot_nt(s.DCKV[at(d), :], weight(1, 0, 384)))
            cross_reduce.second()
    layer_spread.middle()
    s.ST[...] = s.CT[...] + s.AS[at(z), :]
    second_gain = s.GS[pl.ds(z, 1), :]
    for j in range(4):
        users = range(j, min(j + 2, 3) + 1)
        rows = slice(128 * j, 128 * (users[-1] + 1))
        key_parts, value_parts = [], []
        for h in range(3):
            tiles, probs = [], []
            for i in users:
                place = j - max(0, i - 2)
                tiles.append(s.RS[h, i, :, 128 * place : 128 * place + 128])
                probs.append(s.PS[h, i, :, 128 * place : 128 * place + 128].astype(BF16))
            key_parts.append(dot_tn(jnp.concatenate(tiles, axis=0), s.QH[h, rows, :]))
            value_parts.append(dot_tn(jnp.concatenate(probs, axis=0), s.DMH[h, rows, :]))
        merged = jnp.concatenate(key_parts + value_parts, axis=1).astype(BF16)
        s.DQKV[128 * j : 128 * j + 128, 192:576] = merged
    for k in range(2):
        columns = slice(384 * k, 384 * k + 384)
        s.M1[columns, :] = dot_tn(s.SOG[:, columns], s.SM[...]).astype(BF16)
    store_grad(0, 0, [(s.FI, s.DQKV[:, 0:384])])
    store_grad(0, 1, [(s.FI, s.DQKV[:, 384:576]), (None, s.M1)])
    self_reduce = Reduce(0)
    first_sum = Scatter(
        lambda d: dot_nt(s.DQKV[at(d), 0:384], weight(0, 0, 384))
        + dot_nt(s.DQKV[at(d), 384:576], weight(0, 384, 576))
    )
    cross_reduce.third()
    self_reduce.first()
    first_sum.middle()
    memory_sum.middle()

    for h in range(3):
        for k in range(32):
            total = jnp.zeros((1, 128), F32)
            for delta in range(2):
                chosen = jnp.where(s.BK[delta] == k, s.AB[h, delta], 0.0)
                total = total + jnp.sum(chosen, axis=0, keepdims=True)
            if k == 31:
                total = total + jnp.sum(s.AB[h, 2], axis=0, keepdims=True)
            s.BR[32 * h + k : 32 * h + k + 1, :] = total
    sums = lax.dot_general(
        jnp.ones((8, 128), F32),
        s.BR[...],
        (((1,), (1,)), ((), ())),
        precision=lax.Precision.HIGHEST,
        preferred_element_type=F32,
    )
    first_grad = first_sum.total()
    tokens_own = s.TOK[at(z), :].astype(F32)
    token_path, first_gain = norm_back(tokens_own, s.GN[0:1, :], first_grad)
    s.TG[at(z), :] = (s.ST[...] + token_path).astype(BF16)
    token_spread = Spread(s.TG)
    row16 = lax.broadcasted_iota(jnp.int32, (16, 768), 0)
    small = jnp.where(row16 == 0, first_gain, 0.0)
    small = jnp.where(row16 == 1, second_gain, small)
    small = jnp.where(row16 == 2, third_gain, small)
    for h in range(3):
        line = jnp.concatenate([sums[0:1, 32 * h : 32 * h + 32], jnp.zeros((1, 736), F32)], axis=1)
        small = jnp.where(row16 == 3 + 3 * z + h, line, small)

    class Total:
        def __init__(self, buffer, value):
            self.buffer, self.value, self.axis = buffer, value, 0

        def begin(self):
            k = self.axis
            place = (c, z, y, x)[k]
            self.buffer[k, place] = self.value
            ref = self.buffer.at[k, place]
            if k == 0:
                self.ops = [send(ref, ref, to_w=other)]
            elif k == 1:
                self.ops = [send(ref, ref, to_z=mod4(z + d)) for d in (1, 3, 2)]
            elif k == 2:
                self.ops = [send(ref, ref, to_w=wide_at(x, mod4(y + d))) for d in (1, 3, 2)]
            else:
                self.ops = [send(ref, ref, to_w=wide_at(mod4(x + d), y)) for d in (1, 3, 2)]

        def end(self):
            k = self.axis
            for op in self.ops:
                op.wait_recv()
            value = self.buffer[k, 0] + self.buffer[k, 1]
            if k:
                value = value + self.buffer[k, 2] + self.buffer[k, 3]
            self.value = value
            self.axis += 1

    small_sum = Total(s.EX, small)
    small_sum.begin()
    self_reduce.second()
    cross_reduce.fourth()
    small_sum.end()
    small_sum.begin()
    s.MG[at(z), :] = memory_sum.total().astype(BF16)
    memory_spread = Spread(s.MG)
    self_reduce.third()
    token_spread.middle()
    small_sum.end()
    small_sum.begin()
    layer_spread.done()
    move(s.LO, s.lo)
    self_reduce.fourth()
    squares = expand_reduce.squares + shrink_reduce.squares
    squares = squares + cross_reduce.squares + self_reduce.squares
    norm_sum = Total(s.SC, jnp.broadcast_to(jnp.sum(squares), (8, 128)))
    norm_sum.begin()
    small_sum.end()
    small_sum.begin()
    memory_spread.middle()
    norm_sum.end()
    norm_sum.begin()
    for op in (expand_reduce, shrink_reduce, cross_reduce):
        op.done()
    token_spread.done()
    move(s.TG, s.tg)
    norm_sum.end()
    norm_sum.begin()
    small_sum.end()
    s.small[...] = small_sum.value
    small_squares = jnp.sum(small_sum.value * small_sum.value)
    memory_spread.done()
    move(s.MG, s.mg)
    self_reduce.done()
    s.grads[...] = s.RG[...]
    norm_sum.end()
    norm_sum.begin()
    last = {id(op) for op in norm_sum.ops}
    settle([op for op in pending.values() if id(op) not in last])
    norm_sum.end()
    s.norm[...] = jnp.sqrt(norm_sum.value[0:1, 0:1] + small_squares)
    settle(list(pending.values()))
    for op in local[3:]:
        op.wait()


def finish(*refs):
    names = ["tlo", "ttg", "tmg", "grads", "small", "tnorm"] + weight_names + output_names
    s = types.SimpleNamespace(**dict(zip(names, refs)))
    w = lax.axis_index("wide")
    z = lax.axis_index("narrow")
    s.lo[...] = s.tlo[...]
    s.tg[...] = s.ttg[...].astype(F32)
    s.mg[...] = s.tmg[...].astype(F32)
    norm = s.tnorm[...]
    s.norm[...] = norm
    factor = clip_norm / jnp.maximum(norm, clip_norm)

    def update(name, index, gradient):
        group = [getattr(s, name + k) for k in "wms"]
        values = [ref[...] if index is None else ref[index] for ref in group]
        new = adamw(*values, gradient, factor, rate_matrix, decay_matrix)
        for k, value in zip("wms", new):
            ref = getattr(s, name + k + "n")
            if index is None:
                ref[...] = value
            else:
                ref[index] = value

    update("s", 0, s.grads[0, 0, :, 0:192])
    update("s", 1, s.grads[0, 0, :, 192:384])
    update("s", 2, s.grads[0, 1, :, 0:192])
    update("m", 0, s.grads[0, 1, :, 192:384])
    update("c", 1, s.grads[1, 0, :, 0:192])
    update("c", 2, s.grads[1, 0, :, 192:384])
    update("c", 0, s.grads[1, 1, :, 0:192])
    update("m", 1, s.grads[1, 1, :, 192:384])
    update("e", None, jnp.concatenate([s.grads[2, 0], s.grads[2, 1]], axis=1))
    update("h", None, jnp.concatenate([s.grads[3, 0], s.grads[3, 1]], axis=1))

    small = s.small[...]
    pick24 = lax.broadcasted_iota(jnp.int32, (768, 128), 0) == 24 * w + lax.broadcasted_iota(
        jnp.int32, (768, 128), 1
    )
    mine = lax.dot_general(
        small,
        pick24.astype(F32),
        (((1,), (0,)), ((), ())),
        precision=lax.Precision.HIGHEST,
        preferred_element_type=F32,
    )
    new = adamw(s.gw[...], s.gm[...], s.gs[...], mine[0:3, 0:24], factor, rate_small, 0.0)
    s.gwn[...], s.gmn[...], s.gsn[...] = new
    row16 = lax.broadcasted_iota(jnp.int32, (16, 768), 0)
    lane768 = lax.broadcasted_iota(jnp.int32, (16, 768), 1)
    columns = []
    for h in range(3):
        hit = (row16 == 3 + 3 * z + h) & (lane768 == w)
        columns.append(jnp.sum(jnp.where(hit, small, 0.0)).reshape(1, 1))
    bias_grad = jnp.concatenate(columns, axis=1)
    new = adamw(s.bw[...], s.bm[...], s.bs[...], bias_grad, factor, rate_small, 0.0)
    s.bwn[...], s.bmn[...], s.bsn[...] = new


def shards(*args):
    values = dict(zip(input_names, args))

    def turn(value):
        return jnp.swapaxes(value, -1, -2)

    turned = [part + kind for part in "mhb" for kind in "wms"]
    for name in turned:
        values[name] = turn(values[name])
    any_space = pl.BlockSpec(memory_space=pl.ANY)
    vmem = pl.BlockSpec(memory_space=pltpu.VMEM)
    smem = pl.BlockSpec(memory_space=pltpu.SMEM)
    row_shapes = [jax.ShapeDtypeStruct((512, 768), BF16)] * 3
    shapes = row_shapes + [
        jax.ShapeDtypeStruct((4, 2, 24, 384), F32),
        jax.ShapeDtypeStruct((16, 768), F32),
        jax.ShapeDtypeStruct((1, 1), F32),
    ]
    results = pl.pallas_call(
        kernel,
        out_shape=shapes,
        in_specs=[any_space] * 3 + [smem] * 2 + [vmem] * 7,
        out_specs=[any_space] * 3 + [vmem] * 3,
        scratch_shapes=[pltpu.VMEM(shape, kind) for shape, kind in scratch_shapes.values()]
        + [pltpu.SemaphoreType.DMA((count,)) for count in semaphore_shapes.values()],
        compiler_params=pltpu.CompilerParams(
            collective_id=0, has_side_effects=True, vmem_limit_bytes=62 * 1024 * 1024
        ),
    )(*[values[name] for name in step_inputs])
    shapes = [
        jax.ShapeDtypeStruct((512, 768), BF16),
        jax.ShapeDtypeStruct((512, 768), F32),
        jax.ShapeDtypeStruct((512, 768), F32),
        jax.ShapeDtypeStruct((1, 1), F32),
    ]
    for name in weight_names:
        shapes.append(jax.ShapeDtypeStruct(values[name].shape, F32))
    results = pl.pallas_call(
        finish,
        out_shape=shapes,
        in_specs=[vmem] * (6 + len(weight_names)),
        out_specs=[vmem] * len(shapes),
        compiler_params=pltpu.CompilerParams(vmem_limit_bytes=60 * 1024 * 1024),
    )(*results, *[values[name] for name in weight_names])
    out = dict(zip(output_names, results))
    for name in turned:
        out[name + "n"] = turn(out[name + "n"])
    out["norm"] = out["norm"].reshape(())
    return tuple(out[name] for name in output_names)


def solution(mesh):
    rows = P("wide", None)
    attend = P(None, "wide", "narrow")
    merge = P(None, "narrow", "wide")
    expand = P("wide", "narrow")
    shrink = P("narrow", "wide")
    gains = P(None, "wide")
    weights = (attend,) * 6 + (merge,) * 3 + (expand,) * 3 + (shrink,) * 3 + (gains,) * 3
    weights += (P("narrow", "wide"),) * 3
    in_specs = (rows, rows, rows, P("wide"), P("wide")) + weights
    out_specs = (rows, rows, rows, P()) + weights
    return jax.shard_map(shards, mesh=mesh, in_specs=in_specs, out_specs=out_specs, check_vma=False)
```

```python
import math
import types

import jax
import jax.numpy as jnp
from jax import lax
from jax.experimental import pallas as pl
from jax.experimental.pallas import tpu as pltpu
from jax.sharding import PartitionSpec as P

F32 = jnp.float32
BF16 = jnp.bfloat16
MESH = pl.DeviceIdType.MESH
STEP = 10
bucket_edges = (19, 21, 24, 27, 31, 35, 40, 46, 52, 59, 67, 77, 87, 99, 113)
epsilon = 1e-06
negative = -1e30
beta_one = 0.9
beta_two = 0.999
adam_epsilon = 1e-08
clip_norm = 1.0
rate_matrix = 0.03
rate_small = 1.0
decay_matrix = 0.01
SCALE = 0.125
COPIES = 384

weight_names = [part + kind for part in "scmehgb" for kind in "wms"]
input_names = ["tokens", "memory", "cot", "lens", "mlens"] + weight_names
output_names = ["lo", "tg", "mg", "norm"] + [name + "n" for name in weight_names]
step_inputs = ["tokens", "memory", "cot", "lens", "mlens"] + [part + "w" for part in "scmehgb"]
step_outputs = ["lo", "tg", "mg", "grads", "small", "norm"]

scratch_shapes = dict(
    pk=((2, 24, 2112), F32),
    cat=((2, 24, 2112), F32),
    ZS=((4, 48, 576), BF16),
    W=((7, 16, 48, 768), BF16),
    GN=((8, 768), F32),
    GS=((8, 768), F32),
    DC=((512, 128), jnp.int32),
    DR=((8, 512), jnp.int32),
    MR=((8, 512), jnp.int32),
    TOK=((512, 768), BF16),
    MEM=((512, 768), BF16),
    FG=((512, 768), BF16),
    FI=((512, 768), BF16),
    SI=((512, 768), BF16),
    TI=((512, 768), BF16),
    COG=((512, 768), BF16),
    LO=((512, 768), BF16),
    TG=((512, 768), BF16),
    MG=((512, 768), BF16),
    QH=((3, 512, 64), BF16),
    KH=((3, 512, 64), BF16),
    VH=((3, 512, 64), BF16),
    CQH=((3, 512, 64), BF16),
    CKH=((3, 512, 64), BF16),
    CVH=((3, 512, 64), BF16),
    DMH=((3, 512, 64), BF16),
    CDMH=((3, 512, 64), BF16),
    SM=((512, 192), BF16),
    CM=((512, 192), BF16),
    M0=((768, 192), BF16),
    M1=((768, 192), BF16),
    D4=((4, 64, 384), BF16),
    DMX=((4, 64, 384), BF16),
    SMF=((4, 4, 64, 384), BF16),
    CMF=((4, 4, 64, 384), BF16),
    DQF=((4, 4, 64, 384), BF16),
    T=((3, 2, 128, 128), F32),
    BK=((2, 128, 128), jnp.int32),
    PS=((3, 4, 128, 384), F32),
    PC=((3, 512, 512), F32),
    RS=((3, 4, 128, 384), BF16),
    RC=((3, 512, 512), BF16),
    AGR=((512, 768), F32),
    ACT=((512, 768), BF16),
    HG=((512, 768), BF16),
    DCQ=((512, 192), BF16),
    DCKV=((512, 384), BF16),
    DQKV=((512, 576), BF16),
    AS=((512, 768), F32),
    AC=((128, 768), F32),
    CT=((128, 768), F32),
    ST=((128, 768), F32),
    AB=((3, 3, 128, 128), F32),
    BR=((96, 128), F32),
    zsend=((2, 3, 128, 768), BF16),
    zrelay=((2, 2, 64, 768), BF16),
    zrecv=((4, 3, 128, 768), BF16),
    zown=((3, 128, 768), F32),
    ztmp=((2, 2, 64, 768), F32),
    GB=((2, 16, 48, 768), BF16),
    RB=((4, 16, 48, 384), BF16),
    HF=((2, 16, 48, 384), F32),
    HB=((2, 16, 48, 384), BF16),
    RV=((4, 3, 4, 48, 384), BF16),
    RVS=((15, 48, 384), BF16),
    CB=((4, 4, 48, 384), BF16),
    RCV=((4, 4, 48, 384), BF16),
    FN=((4, 2, 24, 384), F32),
    RG=((4, 2, 24, 384), F32),
    EX=((24, 24, 128), F32),
    SC=((24, 8, 128), F32),
)
semaphore_shapes = dict(ssem=COPIES, rsem=COPIES, lsem=8)


def dot(a, b):
    return jnp.dot(a, b, preferred_element_type=F32)


def dot_nt(a, b):
    return lax.dot_general(a, b, (((1,), (1,)), ((), ())), preferred_element_type=F32)


def dot_tn(a, b):
    return lax.dot_general(a, b, (((0,), (0,)), ((), ())), preferred_element_type=F32)


def mod4(v):
    return lax.rem(v + 4, 4)


def mult(v, n):
    return pl.multiple_of(v, n)


def norm_parts(value):
    scale = lax.rsqrt(jnp.mean(value * value, axis=-1, keepdims=True) + epsilon)
    return scale, value * scale


def norm_back(value, gain_row, grad):
    scale, unit = norm_parts(value)
    gain_grad = jnp.sum(grad * unit, axis=0, keepdims=True)
    inner = grad * gain_row
    value_grad = scale * (inner - unit * jnp.mean(inner * unit, axis=-1, keepdims=True))
    return value_grad, gain_grad


def softmax(scores):
    top = jnp.max(scores, axis=-1, keepdims=True)
    exponent = jnp.exp(scores - top)
    return exponent * (1.0 / jnp.sum(exponent, axis=-1, keepdims=True))


def adamw(weight, moment, square, gradient, factor, rate, decay):
    clipped = gradient * factor
    moment_new = beta_one * moment + (1.0 - beta_one) * clipped
    square_new = beta_two * square + (1.0 - beta_two) * clipped * clipped
    corrected = moment_new / (1.0 - beta_one**STEP)
    scaled = square_new / (1.0 - beta_two**STEP)
    weight_new = weight - rate * (corrected / (jnp.sqrt(scaled) + adam_epsilon) + decay * weight)
    return (weight_new, moment_new, square_new)


def kernel(*refs):
    names = step_inputs + step_outputs + list(scratch_shapes) + list(semaphore_shapes)
    s = types.SimpleNamespace(**dict(zip(names, refs)))
    w = lax.axis_index("wide")
    z = lax.axis_index("narrow")
    c = lax.rem(w, 2)
    y = lax.rem(lax.div(w, 2), 4)
    x = lax.div(w, 8)
    other = w + 1 - 2 * c
    zl, zr, zf = mod4(z - 1), mod4(z + 1), mod4(z + 2)
    p1 = x * (1 - c) + y * c
    p2 = y * (1 - c) + x * c
    s1, s2 = 4 - 3 * c, 1 + 3 * c

    def chip(a, b):
        return s1 * a + s2 * b

    def dev(a, b):
        return 2 * chip(a, b) + c

    def wide_at(xx, yy):
        return (xx * 4 + yy) * 2 + c

    started = []
    pending = {}
    local = []

    def move(src, dst):
        op = pltpu.make_async_copy(src, dst, s.lsem.at[len(local)])
        op.start()
        local.append(op)
        return op

    def settle(ops):
        for op in ops:
            op.wait_send()
            del pending[id(op)]

    def send(src, dst, to_w=None, to_z=None):
        slot = len(started)
        assert slot < COPIES
        op = pltpu.make_async_remote_copy(
            src_ref=src,
            dst_ref=dst,
            send_sem=s.ssem.at[slot],
            recv_sem=s.rsem.at[slot],
            device_id=(w if to_w is None else to_w, z if to_z is None else to_z),
            device_id_type=MESH,
        )
        op.start()
        started.append(op)
        pending[id(op)] = op
        return op

    barrier = pltpu.get_barrier_semaphore()
    plane = [(i, j) for i in range(4) for j in range(4) if (i, j) != (0, 0)]
    chip_line = [(other, z)] + [(to, mod4(z + d)) for d in (1, 3, 2) for to in (w, other)]
    peers = chip_line + [(wide_at(mod4(x + i), mod4(y + j)), z) for i, j in plane]
    for peer in peers:
        pl.semaphore_signal(barrier, inc=1, device_id=peer, device_id_type=MESH)

    loads = [move(s.tokens, s.TOK), move(s.cot, s.FG), move(s.memory, s.MEM)]

    lane = lax.broadcasted_iota(jnp.int32, (24, 128), 1)
    row24 = lax.broadcasted_iota(jnp.int32, (24, 128), 0)
    pick = lax.broadcasted_iota(jnp.int32, (24, 24), 0) == lax.broadcasted_iota(
        jnp.int32, (24, 24), 1
    )
    extra = jnp.zeros((24, 128), F32)
    for k in range(3):
        gain = s.gw[k : k + 1, :]
        column = jnp.sum(jnp.where(pick, gain, 0.0), axis=1, keepdims=True)
        extra = jnp.where(lane == k, column, extra)
        extra = jnp.where((lane == 3 + k) & (row24 == 0), s.bw[0:1, k : k + 1], extra)
    for h in range(2):
        s.pk[h, :, 768:1152] = s.ew[:, 384 * h : 384 * h + 384]
        s.pk[h, :, 1152:1536] = s.hw[:, 384 * h : 384 * h + 384]
        s.pk[h, :, 1536:2112] = jnp.concatenate([s.mw[0], s.mw[1], s.cw[0]], axis=1)
    s.pk[0, :, 0:384] = jnp.concatenate([s.sw[0], s.sw[1]], axis=1)
    s.pk[1, :, 0:384] = jnp.concatenate([s.sw[2], extra, jnp.zeros((24, 64), F32)], axis=1)
    s.pk[0, :, 384:768] = jnp.concatenate([s.cw[1], s.cw[2]], axis=1)
    s.pk[1, :, 384:768] = jnp.concatenate([s.cw[0], jnp.zeros((24, 192), F32)], axis=1)

    pl.semaphore_wait(barrier, len(peers))
    pair = send(s.pk.at[1 - c], s.cat.at[c], to_w=other)
    s.cat[c] = s.pk[c]

    row_col = lax.broadcasted_iota(jnp.int32, (512, 128), 0)
    row_row = lax.broadcasted_iota(jnp.int32, (8, 512), 1)
    doc_col = jnp.zeros((512, 128), jnp.int32)
    doc_row = jnp.zeros((8, 512), jnp.int32)
    mem_row = jnp.zeros((8, 512), jnp.int32)
    end, mem_end = jnp.int32(0), jnp.int32(0)
    for k in range(8):
        end = end + s.lens[k]
        mem_end = mem_end + s.mlens[k]
        doc_col = doc_col + (row_col >= end).astype(jnp.int32)
        doc_row = doc_row + (row_row >= end).astype(jnp.int32)
        mem_row = mem_row + (row_row >= mem_end).astype(jnp.int32)
    s.DC[...] = doc_col
    s.DR[...] = doc_row
    s.MR[...] = jnp.where(mem_row < 8, mem_row, -1)
    pair.wait_recv()
    block = s.cat[...].reshape(48, 2112).astype(BF16)
    me = chip(p1, p2)
    c384 = mult(384 * c, 128)
    o384 = mult(384 * (1 - c), 128)
    for g in range(4):
        s.W[g, me, :, pl.ds(c384, 384)] = block[:, 384 * g : 384 * g + 384]

    def block_at(g, index):
        return s.W.at[g, index, :, pl.ds(c384, 384)]

    class Gather:
        def __init__(self, g, eager=False):
            self.g, self.eager, self.four = g, eager, []
            ref = block_at(g, me)
            self.one = {d: send(ref, ref, to_w=dev(mod4(p1 + d), p2)) for d in (1, 3, 2)}

        def share(self, ref):
            self.four.append(send(ref, ref, to_w=other))

        def second(self):
            self.two = {}
            for r, d in ((0, None), (3, 1), (1, 3), (2, 2)):
                if d is not None:
                    self.one[d].wait_recv()
                ref = block_at(self.g, chip(mod4(p1 + r), p2))
                for e in (1, 3, 2):
                    self.two[r, e] = send(ref, ref, to_w=dev(p1, mod4(p2 + e)))
                if self.eager:
                    self.share(ref)

        def third(self):
            for (r, e), op in self.two.items():
                op.wait_recv()
                if self.eager:
                    self.share(block_at(self.g, chip(mod4(p1 + r), mod4(p2 - e))))
            if not self.eager:
                self.share(s.W.at[self.g, :, :, pl.ds(c384, 384)])

        def done(self):
            for op in self.four:
                op.wait_recv()

    gather = {0: Gather(0, True)}
    s.ZS[z] = block[:, 1536:2112]
    stage = [send(s.ZS.at[z], s.ZS.at[z], to_z=to) for to in (zr, zl, zf)]
    gather[1] = Gather(1)
    gather[0].second()
    for op in stage:
        op.wait_recv()
    for k, g in enumerate((4, 5, 6)):
        piece = slice(192 * k, 192 * k + 192)
        two_parts = [s.ZS[2 * c, :, piece], s.ZS[2 * c + 1, :, piece]]
        s.W[g, me, :, pl.ds(c384, 384)] = jnp.concatenate(two_parts, axis=1)
    gather[4] = Gather(4)
    loads[1].wait()
    for t in range(4):
        rows = pl.ds(128 * t, 128)
        seed = jnp.where(s.DC[rows, 0:1] < 8, s.FG[rows, :].astype(F32), 0.0)
        s.FG[rows, :] = seed.astype(BF16)
    loads[0].wait()
    loads[2].wait()

    tile_row = lax.broadcasted_iota(jnp.int32, (128, 128), 0)
    tile_col = lax.broadcasted_iota(jnp.int32, (128, 128), 1)
    for delta in range(2):
        distance = jnp.maximum(128 * delta + tile_row - tile_col, 0)
        bucket = jnp.minimum(distance, 16)
        for edge in bucket_edges:
            bucket = bucket + (distance >= edge).astype(jnp.int32)
        s.BK[delta] = bucket

    gather[0].third()
    gather[4].second()
    gather[1].second()
    for g in (5, 3, 2, 6):
        gather[g] = Gather(g)
    gather[0].done()

    eye = (
        lax.broadcasted_iota(jnp.int32, (8, 256), 0) + 64
        == lax.broadcasted_iota(jnp.int32, (8, 256), 1)
    ).astype(BF16)
    gains = dot_nt(eye, s.W[0, :, :, 512:768].reshape(768, 256))
    s.GN[...] = gains
    last_bias = []
    for h in range(3):
        entry = [gains[3 + h : 4 + h, 24 * k : 24 * k + 1] for k in range(32)]
        last_bias.append(entry[31])
        for delta in range(2):
            bucket = s.BK[delta]
            tile = jnp.broadcast_to(entry[0], (128, 128))
            for k in range(1, 32):
                tile = jnp.where(bucket >= k, entry[k], tile)
            s.T[h, delta] = tile

    for t in range(4):
        rows = pl.ds(128 * t, 128)
        _, unit = norm_parts(s.TOK[rows, :].astype(F32))
        s.FI[rows, :] = (unit * gains[0:1]).astype(BF16)

    def weight(g, start, stop):
        return s.W[g, :, :, start:stop].reshape(768, stop - start)

    query_key = dot(s.FI[...], weight(0, 0, 384))
    for h in range(3):
        s.QH[h] = query_key[:, 64 * h : 64 * h + 64].astype(BF16)
        s.KH[h] = query_key[:, 192 + 64 * h : 256 + 64 * h].astype(BF16)
    value_rows = dot(s.FI[...], weight(0, 384, 576))
    for h in range(3):
        s.VH[h] = value_rows[:, 64 * h : 64 * h + 64].astype(BF16)

    def band(i):
        low = max(0, i - 2)
        return slice(128 * low, 128 * (i + 1)), i - low + 1

    def pack(value):
        return jnp.concatenate([value[0:64], value[64:128]], axis=1)

    def unpack(value):
        return jnp.concatenate([value[:, 0:192], value[:, 192:384]], axis=0)

    class TileSpread:
        def __init__(self, buffer):
            self.buffer, self.ops = buffer, {}

        def send(self, k, tile, value):
            self.buffer[z, tile] = pack(value)
            ref = self.buffer.at[z, tile]
            self.ops[k] = [send(ref, ref, to_z=to) for to in (zf, zr, zl)]

        def done(self, k):
            for op in self.ops[k]:
                op.wait_recv()

        def rows(self, tile):
            parts = [self.buffer[k, tile] for k in range(4)]
            top = jnp.concatenate([part[:, 0:192] for part in parts], axis=1)
            bottom = jnp.concatenate([part[:, 192:384] for part in parts], axis=1)
            return jnp.concatenate([top, bottom], axis=0)

    self_spread = TileSpread(s.SMF)
    for i in range(4):
        rows = slice(128 * i, 128 * i + 128)
        keys, count = band(i)
        width = 128 * count
        ahead = lax.broadcasted_iota(jnp.int32, (128, width), 0) - lax.broadcasted_iota(
            jnp.int32, (128, width), 1
        )
        allowed = (s.DC[rows, 0:1] == s.DR[0:1, keys]) & (ahead + 128 * (count - 1) >= 0)
        mixed = []
        for h in range(3):
            tiles = [jnp.broadcast_to(last_bias[h], (128, 128)), s.T[h, 1], s.T[h, 0]][-count:]
            bias = tiles[0] if count == 1 else jnp.concatenate(tiles, axis=1)
            raw = dot_nt(s.QH[h, rows, :], s.KH[h, keys, :])
            probs = softmax(jnp.where(allowed, raw * SCALE + bias, negative))
            s.PS[h, i, :, 0:width] = probs
            mixed.append(dot(probs.astype(BF16), s.VH[h, keys, :]))
        merged = jnp.concatenate(mixed, axis=1).astype(BF16)
        s.SM[rows, :] = merged
        self_spread.send(i, i, merged)
        if i == 0:
            gather[4].third()
        if i == 1:
            gather[1].third()
            gather[5].second()
        if i == 2:
            gather[3].second()

    def at(d):
        return pl.ds(mult(128 * d, 128), 128)

    class Scatter:
        made = []

        def __init__(self, part, relay=True):
            n = self.n = len(Scatter.made)
            self.relayed = relay
            self.sends, self.waits = [], []
            self.rows = rows = (pl.ds(0, 64), pl.ds(64, 64))
            Scatter.made.append(self)
            if n >= 2:
                settle(Scatter.made[n - 2].sends)
            slot = n % 2
            if not relay:
                for k, to in enumerate((zf, zr, zl)):
                    s.zsend[slot, k] = part(to).astype(BF16)
                    self.give(s.zsend.at[slot, k], s.zrecv.at[n, k], to)
                s.zown[slot] = part(z)
                return
            s.zsend[slot, 0] = part(zf).astype(BF16)
            for k, to in enumerate((zr, zl)):
                value = part(to)
                first = value[0:64] if k == 0 else value[64:128]
                second = value[64:128] if k == 0 else value[0:64]
                s.ztmp[slot, k] = first
                s.zsend[slot, 1 + k, rows[1 - k]] = second.astype(BF16)
            s.zown[slot] = part(z)

        def start(self):
            n, slot, rows = self.n, self.n % 2, self.rows
            self.relays = [
                self.give(s.zsend.at[slot, 0, rows[k]], s.zrelay.at[n - 1, k], to, False)
                for k, to in enumerate((zr, zl))
            ]
            for k, to in enumerate((zr, zl)):
                self.give(s.zsend.at[slot, 1 + k, rows[1 - k]], s.zrecv.at[n, k, rows[1 - k]], to)

        def give(self, src, dst, to, last=True):
            op = send(src, dst, to_z=to)
            self.sends.append(op)
            if last:
                self.waits.append(op)
            return op

        def middle(self):
            n, slot, rows = self.n, self.n % 2, self.rows
            for k, to in enumerate((zr, zl)):
                self.relays[k].wait_recv()
                total = s.ztmp[slot, k] + s.zrelay[n - 1, k].astype(F32)
                s.zsend[slot, 1 + k, rows[k]] = total.astype(BF16)
                self.give(s.zsend.at[slot, 1 + k, rows[k]], s.zrecv.at[n, k, rows[k]], to)

        def total(self):
            for op in self.waits:
                op.wait_recv()
            total = s.zown[self.n % 2]
            for k in range(2 if self.relayed else 3):
                total = total + s.zrecv[self.n, k].astype(F32)
            return total

    class Spread:
        def __init__(self, ref, relay=True):
            self.ref = ref
            mine = ref.at[at(z)]
            self.ops = [send(mine, mine, to_z=to) for to in ((zr, zl) if relay else (zf, zr, zl))]

        def middle(self):
            from_l, from_r = self.ops
            for op, d, start, to in ((from_l, zl, 0, zr), (from_r, zr, 64, zl)):
                op.wait_recv()
                ref = self.ref.at[pl.ds(mult(128 * d + start, 64), 64)]
                self.ops.append(send(ref, ref, to_z=to))

        def done(self):
            for op in self.ops[2:] if len(self.ops) == 4 else self.ops:
                op.wait_recv()

    def own_heads(g):
        half = s.W[g, :, :, pl.ds(mult(384 * lax.div(z, 2), 128), 384)].reshape(768, 384)
        return jnp.where(lax.rem(z, 2) == 0, half[:, 0:192], half[:, 192:384])

    gather[1].done()
    keys_values = dot(s.MEM[...], weight(1, 0, 384))
    for h in range(3):
        s.CKH[h] = keys_values[:, 64 * h : 64 * h + 64].astype(BF16)
        s.CVH[h] = keys_values[:, 192 + 64 * h : 256 + 64 * h].astype(BF16)
    gather[4].done()
    cross_spread = TileSpread(s.CMF)
    for i in range(4):
        rows = slice(128 * i, 128 * i + 128)
        self_spread.done(i)
        after_self = s.TOK[rows, :].astype(F32) + dot_nt(self_spread.rows(i), weight(4, 0, 768))
        s.AS[rows, :] = after_self
        second_in = (norm_parts(after_self)[1] * s.GN[1:2, :]).astype(BF16)
        s.SI[rows, :] = second_in
        queries = dot(second_in, weight(1, 384, 576)).astype(BF16)
        allowed = s.DC[rows, 0:1] == s.MR[0:1, :]
        mixed = []
        for h in range(3):
            query = queries[:, 64 * h : 64 * h + 64]
            s.CQH[h, rows, :] = query
            raw = dot_nt(query, s.CKH[h])
            probs = softmax(jnp.where(allowed, raw * SCALE, negative))
            s.PC[h, rows, :] = probs
            mixed.append(dot(probs.astype(BF16), s.CVH[h]))
        merged = jnp.concatenate(mixed, axis=1).astype(BF16)
        s.CM[rows, :] = merged
        cross_spread.send(i, i, merged)
        if i == 0:
            gather[5].third()
            gather[2].second()
        if i == 1:
            gather[3].third()
            gather[6].second()
        if i == 2:
            gather[2].third()
    gather[3].done()
    for t in range(2):
        rows = slice(256 * t, 256 * t + 256)
        s.AGR[rows, :] = dot(s.FG[rows, :], weight(3, 0, 768))
    gather[5].done()
    gather[6].third()

    def cross_merge(tile, rows):
        return s.AS[rows, :] + dot_nt(cross_spread.rows(tile), weight(5, 0, 768))

    for i in range(4):
        rows = slice(128 * i, 128 * i + 128)
        cross_spread.done(i)
        s.TI[rows, :] = (norm_parts(cross_merge(i, rows))[1] * s.GN[2:3, :]).astype(BF16)
    gather[2].done()

    def feed_chunk(d):
        rows = at(d)
        hidden = dot(s.TI[rows, :], weight(2, 0, 768))
        phi = 0.5 + 0.5 * lax.erf(hidden * math.sqrt(0.5))
        slope = phi + hidden * jnp.exp(-0.5 * hidden * hidden) * (1.0 / math.sqrt(2.0 * math.pi))
        s.ACT[rows, :] = (hidden * phi).astype(BF16)
        hidden_grad = (s.AGR[rows, :] * slope).astype(BF16)
        s.HG[rows, :] = hidden_grad
        return dot_nt(hidden_grad, weight(2, 0, 768))

    third_sum = Scatter(feed_chunk, relay=False)

    grad_place = {2: 0, 3: 1, 1: 0, 0: 1}
    held = {}

    def store_grad(g, half, pairs):
        place = grad_place[g]
        if place in held and held[place].g != g and id(held[place].pair) in pending:
            settle([held[place].pair])
        for k in range(2):
            columns = slice(384 * k, 384 * k + 384)
            values = [
                right[columns, :] if left is None else dot_tn(left[:, columns], right).astype(BF16)
                for left, right in pairs
            ]
            value = values[0] if len(values) == 1 else jnp.concatenate(values, axis=1)
            s.GB[place, 8 * k : 8 * k + 8, :, 384 * half : 384 * half + 384] = value.reshape(
                8, 48, 384
            )

    def block_sum(a, b):
        return a.astype(F32) + b.astype(F32)

    class Reduce:
        def __init__(self, g):
            self.g = g
            self.place = grad_place[g]
            self.total = s.HF.at[self.place]
            self.low = s.HB.at[self.place]
            self.pair = send(s.GB.at[self.place, :, :, pl.ds(o384, 384)], s.RB.at[g], to_w=other)

        def first(self):
            g = self.g
            self.pair.wait_recv()
            if self.place in held:
                old = held[self.place]
                settle(list(old.ops.values()))
            held[self.place] = self
            total = block_sum(s.GB[self.place, :, :, pl.ds(c384, 384)], s.RB[g])
            self.total[...] = total
            self.low[...] = total.astype(BF16)
            self.ops = {}
            if g == 0:
                for k, (i, j) in enumerate(plane):
                    xx, yy = mod4(x + i), mod4(y + j)
                    self.ops[k] = send(self.low.at[4 * xx + yy], s.RVS.at[k], to_w=wide_at(xx, yy))
                return
            for e in (1, 3, 2):
                for r in range(4):
                    self.ops[e, r] = send(
                        self.low.at[chip(mod4(p1 + r), mod4(p2 + e))],
                        s.RV.at[g, e - 1, r],
                        to_w=dev(p1, mod4(p2 + e)),
                    )

        def second(self):
            g = self.g
            self.last = {}
            for r in (1, 3, 2, 0):
                total = self.total[chip(mod4(p1 + r), p2)]
                for e in (1, 3, 2):
                    self.ops[e, r].wait_recv()
                    total = total + s.RV[g, e - 1, r].astype(F32)
                if r:
                    s.CB[g, r] = total.astype(BF16)
                    self.last[r] = send(s.CB.at[g, r], s.RCV.at[g, r], to_w=dev(mod4(p1 + r), p2))
                else:
                    self.kept = total

        def third(self):
            g = self.g
            if g == 0:
                total = self.total[4 * x + y]
                for k in range(15):
                    self.ops[k].wait_recv()
                    total = total + s.RVS[k].astype(F32)
            else:
                total = self.kept
                for r in (1, 3, 2):
                    self.last[r].wait_recv()
                    total = total + s.RCV[g, r].astype(F32)
            self.squares = jnp.sum(total * total, axis=0, keepdims=True)
            s.FN[g, 0] = total[0:24]
            s.FN[g, 1] = total[24:48]
            s.RG[g, c] = s.FN[g, c]
            self.give = send(s.FN.at[g, 1 - c], s.RG.at[g, c], to_w=other)

        def done(self):
            self.give.wait_recv()

    def two_halves(g, left, right):
        for half in range(2):
            store_grad(g, half, [(left, right[:, 384 * half : 384 * half + 384])])

    two_halves(2, s.TI, s.HG)
    expand_reduce = Reduce(2)
    feed_sum = Scatter(lambda d: dot_nt(s.ACT[at(d), :], weight(3, 0, 768)))
    feed_sum.start()
    after_cross = cross_merge(z, at(z))
    s.AC[...] = after_cross
    s.M0[...] = own_heads(4)
    two_halves(3, s.FG, s.ACT)
    shrink_reduce = Reduce(3)
    third_grad = third_sum.total()
    cross_path, third_gain = norm_back(s.AC[...], s.GN[2:3, :], third_grad)
    cross_total = s.FG[at(z), :].astype(F32) + cross_path
    cross_out = cross_total.astype(BF16)
    mixed_all = dot(cross_out, weight(5, 0, 768)).astype(BF16)
    for k in range(4):
        s.D4[k] = pack(mixed_all[:, 192 * k : 192 * k + 192])
    s.DMX[z] = s.D4[z]
    mixed_ops = {to: send(s.D4.at[d], s.DMX.at[z], to_z=d) for to, d in enumerate((zr, zl, zf))}
    s.CT[...] = cross_total
    s.COG[at(z), :] = cross_out
    spread = Spread(s.COG)
    expand_reduce.first()
    feed_sum.middle()
    shrink_reduce.first()
    query_spread = TileSpread(s.DQF)
    for op in mixed_ops.values():
        op.wait_recv()

    def cross_back(d):
        rows = slice(128 * d, 128 * d + 128)
        grad = unpack(s.DMX[d])
        parts = []
        for h in range(3):
            mixed_grad = grad[:, 64 * h : 64 * h + 64]
            s.CDMH[h, rows, :] = mixed_grad
            probs_grad = dot_nt(mixed_grad, s.CVH[h])
            probs = s.PC[h, rows, :]
            inner = jnp.sum(probs * probs_grad, axis=-1, keepdims=True)
            raw = (probs * (probs_grad - inner) * SCALE).astype(BF16)
            s.RC[h, rows, :] = raw
            parts.append(dot(raw, s.CKH[h]))
        merged = jnp.concatenate(parts, axis=1).astype(BF16)
        s.DCQ[rows, :] = merged
        query_spread.send(d, d, merged)

    cross_back(3)
    cross_back(2)
    cross_back(1)
    spread.middle()
    cross_back(0)
    parts = [dot_tn(s.RC[h], s.CQH[h]) for h in range(3)]
    parts += [dot_tn(s.PC[h].astype(BF16), s.CDMH[h]) for h in range(3)]
    s.DCKV[...] = jnp.concatenate(parts, axis=1).astype(BF16)
    expand_reduce.second()
    store_grad(1, 0, [(s.MEM, s.DCKV[...])])
    memory_sum = Scatter(lambda d: dot_nt(s.DCKV[at(d), :], weight(1, 0, 384)))
    shrink_reduce.second()
    gather[6].done()
    spread.done()
    memory_sum.start()

    s.SOG = s.TI
    for i in (3, 2, 1, 0):
        rows = slice(128 * i, 128 * i + 128)
        query_spread.done(i)
        second_grad = dot_nt(query_spread.rows(i), weight(6, 0, 768))
        self_path, second_gain = norm_back(s.AS[rows, :], s.GN[1:2, :], second_grad)
        s.AS[rows, :] = self_path
        s.GS[i : i + 1, :] = second_gain
        self_out = (s.COG[rows, :].astype(F32) + self_path).astype(BF16)
        s.SOG[rows, :] = self_out
        keys, count = band(i)
        width = 128 * count
        grad = dot(self_out, s.M0[...]).astype(BF16)
        parts = []
        for h in range(3):
            mixed_grad = grad[:, 64 * h : 64 * h + 64]
            s.DMH[h, rows, :] = mixed_grad
            probs_grad = dot_nt(mixed_grad, s.VH[h, keys, :])
            probs = s.PS[h, i, :, 0:width]
            inner = jnp.sum(probs * probs_grad, axis=-1, keepdims=True)
            score_grad = probs * (probs_grad - inner)
            for t in range(count):
                delta = count - 1 - t
                tile = score_grad[:, 128 * t : 128 * t + 128]
                if i == 3:
                    s.AB[h, delta] = tile
                else:
                    s.AB[h, delta] += tile
            raw = (score_grad * SCALE).astype(BF16)
            s.RS[h, i, :, 0:width] = raw
            parts.append(dot(raw, s.KH[h, keys, :]))
        s.DQKV[rows, 0:192] = jnp.concatenate(parts, axis=1).astype(BF16)

        users = range(i, min(i + 2, 3) + 1)
        span = slice(128 * i, 128 * (users[-1] + 1))
        key_parts, value_parts = [], []
        for h in range(3):
            tiles, probs = [], []
            for user in users:
                place = i - max(0, user - 2)
                tiles.append(s.RS[h, user, :, 128 * place : 128 * place + 128])
                probs.append(s.PS[h, user, :, 128 * place : 128 * place + 128].astype(BF16))
            key_parts.append(dot_tn(jnp.concatenate(tiles, axis=0), s.QH[h, span, :]))
            value_parts.append(dot_tn(jnp.concatenate(probs, axis=0), s.DMH[h, span, :]))
        s.DQKV[rows, 192:576] = jnp.concatenate(key_parts + value_parts, axis=1).astype(BF16)

        if i == 3:
            layer_rows = s.AC[...] + feed_sum.total()
            layer_rows = jnp.where(s.DC[at(z), 0:1] < 8, layer_rows, 0.0)
            s.LO[at(z), :] = layer_rows.astype(BF16)
            layer_spread = Spread(s.LO)
        if i == 2:
            store_grad(1, 1, [(s.SI, s.DCQ[...]), (s.COG, s.CM[...])])
            cross_reduce = Reduce(1)
            expand_reduce.third()
        if i == 1:
            cross_reduce.first()
        if i == 0:
            memory_sum.middle()
    shrink_reduce.third()
    s.ST[...] = s.CT[...] + s.AS[at(z), :]
    second_gain = s.GS[pl.ds(z, 1), :]
    first_gains = []

    def first_part(d):
        rows = at(d)
        part = dot_nt(s.DQKV[rows, 0:384], weight(0, 0, 384))
        part = part + dot_nt(s.DQKV[rows, 384:576], weight(0, 384, 576))
        unit = norm_parts(s.TOK[rows, :].astype(F32))[1]
        first_gains.append(jnp.sum(part * unit, axis=0, keepdims=True))
        return part

    first_sum = Scatter(first_part, relay=False)
    first_gain = sum(first_gains)
    for k in range(2):
        columns = slice(384 * k, 384 * k + 384)
        s.M1[columns, :] = dot_tn(s.SOG[:, columns], s.SM[...]).astype(BF16)
    store_grad(0, 0, [(s.FI, s.DQKV[:, 0:384])])
    store_grad(0, 1, [(s.FI, s.DQKV[:, 384:576]), (None, s.M1)])
    self_reduce = Reduce(0)
    layer_spread.middle()

    for h in range(3):
        for k in range(32):
            total = jnp.zeros((1, 128), F32)
            for delta in range(2):
                chosen = jnp.where(s.BK[delta] == k, s.AB[h, delta], 0.0)
                total = total + jnp.sum(chosen, axis=0, keepdims=True)
            if k == 31:
                total = total + jnp.sum(s.AB[h, 2], axis=0, keepdims=True)
            s.BR[32 * h + k : 32 * h + k + 1, :] = total
    sums = lax.dot_general(
        jnp.ones((8, 128), F32),
        s.BR[...],
        (((1,), (1,)), ((), ())),
        precision=lax.Precision.HIGHEST,
        preferred_element_type=F32,
    )
    self_reduce.first()

    class Total:
        def __init__(self, buffer, value):
            self.buffer = buffer
            place = 4 * c + z
            buffer[place] = value
            self.ops = [send(buffer.at[place], buffer.at[place], *peer) for peer in chip_line]

        def add(self, start, count):
            for op in self.ops:
                op.wait_recv()
            value = self.buffer[start]
            for k in range(1, count):
                value = value + self.buffer[start + k]
            return value

        def second(self):
            value = self.add(0, 8)
            place = 8 + 4 * x + y
            self.buffer[place] = value
            ref = self.buffer.at[place]
            self.ops = [
                send(ref, ref, to_w=wide_at(mod4(x + i), mod4(y + j))) for i, j in plane
            ]

        def done(self):
            return self.add(8, 16)

    gain_rows = [
        gain[:, 128 * k : 128 * k + 128]
        for gain in (first_gain, second_gain, third_gain)
        for k in range(6)
    ]
    line = jnp.concatenate([sums[0:1, :], jnp.zeros((1, 32), F32)], axis=1)
    bias_rows = [jnp.where(z == k, line, 0.0) for k in range(4)]
    small = jnp.concatenate(gain_rows + bias_rows + [jnp.zeros((2, 128), F32)], axis=0)
    small_sum = Total(s.EX, small)
    s.MG[at(z), :] = memory_sum.total().astype(BF16)
    memory_spread = Spread(s.MG)
    cross_reduce.second()
    first_grad = first_sum.total()
    token_path, _ = norm_back(s.TOK[at(z), :].astype(F32), s.GN[0:1, :], first_grad)
    s.TG[at(z), :] = (s.ST[...] + token_path).astype(BF16)
    token_spread = Spread(s.TG, relay=False)
    small_sum.second()
    memory_spread.middle()
    cross_reduce.third()
    self_reduce.third()
    squares = expand_reduce.squares + shrink_reduce.squares
    squares = squares + cross_reduce.squares + self_reduce.squares
    norm_sum = Total(s.SC, jnp.broadcast_to(jnp.sum(squares), (8, 128)))
    layer_spread.done()
    move(s.LO, s.lo)
    for op in (expand_reduce, shrink_reduce, cross_reduce):
        op.done()
    small = small_sum.done()
    s.small[...] = small
    small_squares = jnp.sum(small * small)
    norm_sum.second()
    self_reduce.done()
    s.grads[...] = s.RG[...]
    memory_spread.done()
    move(s.MG, s.mg)
    token_spread.done()
    move(s.TG, s.tg)
    last = {id(op) for op in norm_sum.ops}
    settle([op for op in pending.values() if id(op) not in last])
    s.norm[...] = jnp.sqrt(norm_sum.done()[0:1, 0:1] + small_squares)
    settle(list(pending.values()))
    for op in local[3:]:
        op.wait()


def finish(*refs):
    names = ["tlo", "ttg", "tmg", "grads", "small", "tnorm"] + weight_names + output_names
    s = types.SimpleNamespace(**dict(zip(names, refs)))
    w = lax.axis_index("wide")
    z = lax.axis_index("narrow")
    s.lo[...] = s.tlo[...]
    s.tg[...] = s.ttg[...].astype(F32)
    s.mg[...] = s.tmg[...].astype(F32)
    norm = s.tnorm[...]
    s.norm[...] = norm
    factor = clip_norm / jnp.maximum(norm, clip_norm)

    def update(name, index, gradient):
        group = [getattr(s, name + k) for k in "wms"]
        values = [ref[...] if index is None else ref[index] for ref in group]
        new = adamw(*values, gradient, factor, rate_matrix, decay_matrix)
        for k, value in zip("wms", new):
            ref = getattr(s, name + k + "n")
            if index is None:
                ref[...] = value
            else:
                ref[index] = value

    update("s", 0, s.grads[0, 0, :, 0:192])
    update("s", 1, s.grads[0, 0, :, 192:384])
    update("s", 2, s.grads[0, 1, :, 0:192])
    update("m", 0, s.grads[0, 1, :, 192:384])
    update("c", 1, s.grads[1, 0, :, 0:192])
    update("c", 2, s.grads[1, 0, :, 192:384])
    update("c", 0, s.grads[1, 1, :, 0:192])
    update("m", 1, s.grads[1, 1, :, 192:384])
    update("e", None, jnp.concatenate([s.grads[2, 0], s.grads[2, 1]], axis=1))
    update("h", None, jnp.concatenate([s.grads[3, 0], s.grads[3, 1]], axis=1))

    small = s.small[...]
    pick24 = lax.broadcasted_iota(jnp.int32, (768, 128), 0) == 24 * w + lax.broadcasted_iota(
        jnp.int32, (768, 128), 1
    )
    gains = [
        jnp.concatenate([small[6 * k + j : 6 * k + j + 1] for j in range(6)], axis=1)
        for k in range(3)
    ]
    mine = lax.dot_general(
        jnp.concatenate(gains + [jnp.zeros((5, 768), F32)], axis=0),
        pick24.astype(F32),
        (((1,), (0,)), ((), ())),
        precision=lax.Precision.HIGHEST,
        preferred_element_type=F32,
    )
    new = adamw(s.gw[...], s.gm[...], s.gs[...], mine[0:3, 0:24], factor, rate_small, 0.0)
    s.gwn[...], s.gmn[...], s.gsn[...] = new
    row24 = lax.broadcasted_iota(jnp.int32, (24, 128), 0)
    lane = lax.broadcasted_iota(jnp.int32, (24, 128), 1)
    columns = []
    for h in range(3):
        hit = (row24 == 18 + z) & (lane == 32 * h + w)
        columns.append(jnp.sum(jnp.where(hit, small, 0.0)).reshape(1, 1))
    bias_grad = jnp.concatenate(columns, axis=1)
    new = adamw(s.bw[...], s.bm[...], s.bs[...], bias_grad, factor, rate_small, 0.0)
    s.bwn[...], s.bmn[...], s.bsn[...] = new


def shards(*args):
    values = dict(zip(input_names, args))

    def turn(value):
        return jnp.swapaxes(value, -1, -2)

    turned = [part + kind for part in "mhb" for kind in "wms"]
    for name in turned:
        values[name] = turn(values[name])
    any_space = pl.BlockSpec(memory_space=pl.ANY)
    vmem = pl.BlockSpec(memory_space=pltpu.VMEM)
    smem = pl.BlockSpec(memory_space=pltpu.SMEM)
    row_shapes = [jax.ShapeDtypeStruct((512, 768), BF16)] * 3
    shapes = row_shapes + [
        jax.ShapeDtypeStruct((4, 2, 24, 384), F32),
        jax.ShapeDtypeStruct((24, 128), F32),
        jax.ShapeDtypeStruct((1, 1), F32),
    ]
    results = pl.pallas_call(
        kernel,
        out_shape=shapes,
        in_specs=[any_space] * 3 + [smem] * 2 + [vmem] * 7,
        out_specs=[any_space] * 3 + [vmem] * 3,
        scratch_shapes=[pltpu.VMEM(shape, kind) for shape, kind in scratch_shapes.values()]
        + [pltpu.SemaphoreType.DMA((count,)) for count in semaphore_shapes.values()],
        compiler_params=pltpu.CompilerParams(
            collective_id=0, has_side_effects=True, vmem_limit_bytes=62 * 1024 * 1024
        ),
    )(*[values[name] for name in step_inputs])
    shapes = [
        jax.ShapeDtypeStruct((512, 768), BF16),
        jax.ShapeDtypeStruct((512, 768), F32),
        jax.ShapeDtypeStruct((512, 768), F32),
        jax.ShapeDtypeStruct((1, 1), F32),
    ]
    for name in weight_names:
        shapes.append(jax.ShapeDtypeStruct(values[name].shape, F32))
    results = pl.pallas_call(
        finish,
        out_shape=shapes,
        in_specs=[vmem] * (6 + len(weight_names)),
        out_specs=[vmem] * len(shapes),
        compiler_params=pltpu.CompilerParams(vmem_limit_bytes=60 * 1024 * 1024),
    )(*results, *[values[name] for name in weight_names])
    out = dict(zip(output_names, results))
    for name in turned:
        out[name + "n"] = turn(out[name + "n"])
    out["norm"] = out["norm"].reshape(())
    return tuple(out[name] for name in output_names)


def solution(mesh):
    rows = P("wide", None)
    attend = P(None, "wide", "narrow")
    merge = P(None, "narrow", "wide")
    expand = P("wide", "narrow")
    shrink = P("narrow", "wide")
    gains = P(None, "wide")
    weights = (attend,) * 6 + (merge,) * 3 + (expand,) * 3 + (shrink,) * 3 + (gains,) * 3
    weights += (P("narrow", "wide"),) * 3
    in_specs = (rows, rows, rows, P("wide"), P("wide")) + weights
    out_specs = (rows, rows, rows, P()) + weights
    return jax.shard_map(shards, mesh=mesh, in_specs=in_specs, out_specs=out_specs, check_vma=False)
```

```python
import math
import types

import jax
import jax.numpy as jnp
from jax import lax
from jax.experimental import pallas as pl
from jax.experimental.pallas import tpu as pltpu
from jax.sharding import PartitionSpec as P

F32 = jnp.float32
BF16 = jnp.bfloat16
MESH = pl.DeviceIdType.MESH
STEP = 10
bucket_edges = (19, 21, 24, 27, 31, 35, 40, 46, 52, 59, 67, 77, 87, 99, 113)
epsilon = 1e-06
negative = -1e30
beta_one = 0.9
beta_two = 0.999
adam_epsilon = 1e-08
clip_norm = 1.0
rate_matrix = 0.03
rate_small = 1.0
decay_matrix = 0.01
SCALE = 0.125
COPIES = 384

weight_names = [part + kind for part in "scmehgb" for kind in "wms"]
input_names = ["tokens", "memory", "cot", "lens", "mlens"] + weight_names
output_names = ["lo", "tg", "mg", "norm"] + [name + "n" for name in weight_names]
step_inputs = ["tokens", "memory", "cot", "lens", "mlens"] + [part + "w" for part in "scmehgb"]
step_outputs = ["lo", "tg", "mg", "grads", "small", "norm"]

scratch_shapes = dict(
    pk=((2, 24, 2112), F32),
    cat=((2, 24, 2112), F32),
    ZS=((4, 48, 576), BF16),
    W=((7, 16, 48, 768), BF16),
    GN=((8, 768), F32),
    GS=((8, 768), F32),
    DC=((512, 128), jnp.int32),
    DR=((8, 512), jnp.int32),
    MR=((8, 512), jnp.int32),
    TOK=((512, 768), BF16),
    MEM=((512, 768), BF16),
    FG=((512, 768), BF16),
    FI=((512, 768), BF16),
    SI=((512, 768), BF16),
    TI=((512, 768), BF16),
    COG=((512, 768), BF16),
    LO=((512, 768), BF16),
    TG=((512, 768), BF16),
    MG=((512, 768), BF16),
    QH=((3, 512, 64), BF16),
    KH=((3, 512, 64), BF16),
    VH=((3, 512, 64), BF16),
    CQH=((3, 512, 64), BF16),
    CKH=((3, 512, 64), BF16),
    CVH=((3, 512, 64), BF16),
    DMH=((3, 512, 64), BF16),
    CDMH=((3, 512, 64), BF16),
    SM=((512, 192), BF16),
    CM=((512, 192), BF16),
    M0=((768, 192), BF16),
    M1=((768, 192), BF16),
    D4=((4, 64, 384), BF16),
    DMX=((4, 64, 384), BF16),
    SMF=((4, 4, 64, 384), BF16),
    CMF=((4, 4, 64, 384), BF16),
    DQF=((4, 4, 64, 384), BF16),
    T=((3, 2, 128, 128), F32),
    BK=((2, 128, 128), jnp.int32),
    PS=((3, 4, 128, 384), F32),
    PC=((3, 512, 512), F32),
    RS=((3, 4, 128, 384), BF16),
    RC=((3, 512, 512), BF16),
    AGR=((512, 768), F32),
    ACT=((512, 768), BF16),
    HG=((512, 768), BF16),
    DCQ=((512, 192), BF16),
    DCKV=((512, 384), BF16),
    DQKV=((512, 576), BF16),
    AS=((512, 768), F32),
    AC=((128, 768), F32),
    CT=((128, 768), F32),
    ST=((128, 768), F32),
    AB=((3, 3, 128, 128), F32),
    BR=((96, 128), F32),
    zsend=((2, 3, 128, 768), BF16),
    zrelay=((4, 2, 64, 768), BF16),
    zrecv=((4, 3, 128, 768), BF16),
    zown=((3, 128, 768), F32),
    ztmp=((2, 2, 64, 768), F32),
    GB=((2, 16, 48, 768), BF16),
    RB=((4, 16, 48, 384), BF16),
    HF=((2, 16, 48, 384), F32),
    HB=((2, 16, 48, 384), BF16),
    RV=((4, 3, 4, 48, 384), BF16),
    RVS=((15, 48, 384), BF16),
    CB=((4, 4, 48, 384), BF16),
    RCV=((4, 4, 48, 384), BF16),
    FN=((4, 2, 24, 384), F32),
    RG=((4, 2, 24, 384), F32),
    EX=((24, 24, 128), F32),
    SC=((24, 8, 128), F32),
)
semaphore_shapes = dict(ssem=COPIES, rsem=COPIES, lsem=8)


def dot(a, b):
    return jnp.dot(a, b, preferred_element_type=F32)


def dot_nt(a, b):
    return lax.dot_general(a, b, (((1,), (1,)), ((), ())), preferred_element_type=F32)


def dot_tn(a, b):
    return lax.dot_general(a, b, (((0,), (0,)), ((), ())), preferred_element_type=F32)


def mod4(v):
    return lax.rem(v + 4, 4)


def mult(v, n):
    return pl.multiple_of(v, n)


def norm_parts(value):
    scale = lax.rsqrt(jnp.mean(value * value, axis=-1, keepdims=True) + epsilon)
    return scale, value * scale


def norm_back(value, gain_row, grad):
    scale, unit = norm_parts(value)
    gain_grad = jnp.sum(grad * unit, axis=0, keepdims=True)
    inner = grad * gain_row
    value_grad = scale * (inner - unit * jnp.mean(inner * unit, axis=-1, keepdims=True))
    return value_grad, gain_grad


def softmax(scores):
    top = jnp.max(scores, axis=-1, keepdims=True)
    exponent = jnp.exp(scores - top)
    return exponent * (1.0 / jnp.sum(exponent, axis=-1, keepdims=True))


def adamw(weight, moment, square, gradient, factor, rate, decay):
    clipped = gradient * factor
    moment_new = beta_one * moment + (1.0 - beta_one) * clipped
    square_new = beta_two * square + (1.0 - beta_two) * clipped * clipped
    corrected = moment_new / (1.0 - beta_one**STEP)
    scaled = square_new / (1.0 - beta_two**STEP)
    weight_new = weight - rate * (corrected / (jnp.sqrt(scaled) + adam_epsilon) + decay * weight)
    return (weight_new, moment_new, square_new)


def kernel(*refs):
    names = step_inputs + step_outputs + list(scratch_shapes) + list(semaphore_shapes)
    s = types.SimpleNamespace(**dict(zip(names, refs)))
    w = lax.axis_index("wide")
    z = lax.axis_index("narrow")
    c = lax.rem(w, 2)
    y = lax.rem(lax.div(w, 2), 4)
    x = lax.div(w, 8)
    other = w + 1 - 2 * c
    zl, zr, zf = mod4(z - 1), mod4(z + 1), mod4(z + 2)
    p1 = x * (1 - c) + y * c
    p2 = y * (1 - c) + x * c
    s1, s2 = 4 - 3 * c, 1 + 3 * c

    def chip(a, b):
        return s1 * a + s2 * b

    def dev(a, b):
        return 2 * chip(a, b) + c

    def wide_at(xx, yy):
        return (xx * 4 + yy) * 2 + c

    started = []
    pending = {}
    local = []

    def move(src, dst):
        op = pltpu.make_async_copy(src, dst, s.lsem.at[len(local)])
        op.start()
        local.append(op)
        return op

    def settle(ops):
        for op in ops:
            op.wait_send()
            del pending[id(op)]

    def send(src, dst, to_w=None, to_z=None):
        slot = len(started)
        assert slot < COPIES
        op = pltpu.make_async_remote_copy(
            src_ref=src,
            dst_ref=dst,
            send_sem=s.ssem.at[slot],
            recv_sem=s.rsem.at[slot],
            device_id=(w if to_w is None else to_w, z if to_z is None else to_z),
            device_id_type=MESH,
        )
        op.start()
        started.append(op)
        pending[id(op)] = op
        return op

    barrier = pltpu.get_barrier_semaphore()
    plane = [(i, j) for i in range(4) for j in range(4) if (i, j) != (0, 0)]
    chip_line = [(other, z)] + [(to, mod4(z + d)) for d in (1, 3, 2) for to in (w, other)]
    peers = chip_line + [(wide_at(mod4(x + i), mod4(y + j)), z) for i, j in plane]
    for peer in peers:
        pl.semaphore_signal(barrier, inc=1, device_id=peer, device_id_type=MESH)

    loads = [move(s.tokens, s.TOK), move(s.cot, s.FG), move(s.memory, s.MEM)]

    lane = lax.broadcasted_iota(jnp.int32, (24, 128), 1)
    row24 = lax.broadcasted_iota(jnp.int32, (24, 128), 0)
    pick = lax.broadcasted_iota(jnp.int32, (24, 24), 0) == lax.broadcasted_iota(
        jnp.int32, (24, 24), 1
    )
    extra = jnp.zeros((24, 128), F32)
    for k in range(3):
        gain = s.gw[k : k + 1, :]
        column = jnp.sum(jnp.where(pick, gain, 0.0), axis=1, keepdims=True)
        extra = jnp.where(lane == k, column, extra)
        extra = jnp.where((lane == 3 + k) & (row24 == 0), s.bw[0:1, k : k + 1], extra)
    for h in range(2):
        s.pk[h, :, 768:1152] = s.ew[:, 384 * h : 384 * h + 384]
        s.pk[h, :, 1152:1536] = s.hw[:, 384 * h : 384 * h + 384]
        s.pk[h, :, 1536:2112] = jnp.concatenate([s.mw[0], s.mw[1], s.cw[0]], axis=1)
    s.pk[0, :, 0:384] = jnp.concatenate([s.sw[0], s.sw[1]], axis=1)
    s.pk[1, :, 0:384] = jnp.concatenate([s.sw[2], extra, jnp.zeros((24, 64), F32)], axis=1)
    s.pk[0, :, 384:768] = jnp.concatenate([s.cw[1], s.cw[2]], axis=1)
    s.pk[1, :, 384:768] = jnp.concatenate([s.cw[0], jnp.zeros((24, 192), F32)], axis=1)

    pl.semaphore_wait(barrier, len(peers))
    pair = send(s.pk.at[1 - c], s.cat.at[c], to_w=other)
    s.cat[c] = s.pk[c]

    row_col = lax.broadcasted_iota(jnp.int32, (512, 128), 0)
    row_row = lax.broadcasted_iota(jnp.int32, (8, 512), 1)
    doc_col = jnp.zeros((512, 128), jnp.int32)
    doc_row = jnp.zeros((8, 512), jnp.int32)
    mem_row = jnp.zeros((8, 512), jnp.int32)
    end, mem_end = jnp.int32(0), jnp.int32(0)
    for k in range(8):
        end = end + s.lens[k]
        mem_end = mem_end + s.mlens[k]
        doc_col = doc_col + (row_col >= end).astype(jnp.int32)
        doc_row = doc_row + (row_row >= end).astype(jnp.int32)
        mem_row = mem_row + (row_row >= mem_end).astype(jnp.int32)
    s.DC[...] = doc_col
    s.DR[...] = doc_row
    s.MR[...] = jnp.where(mem_row < 8, mem_row, -1)
    pair.wait_recv()
    block = s.cat[...].reshape(48, 2112).astype(BF16)
    me = chip(p1, p2)
    c384 = mult(384 * c, 128)
    o384 = mult(384 * (1 - c), 128)
    for g in range(4):
        s.W[g, me, :, pl.ds(c384, 384)] = block[:, 384 * g : 384 * g + 384]

    def block_at(g, index):
        return s.W.at[g, index, :, pl.ds(c384, 384)]

    class Gather:
        def __init__(self, g, eager=False):
            self.g, self.eager, self.four = g, eager, []
            ref = block_at(g, me)
            self.one = {d: send(ref, ref, to_w=dev(mod4(p1 + d), p2)) for d in (1, 3, 2)}

        def share(self, ref):
            self.four.append(send(ref, ref, to_w=other))

        def second(self):
            self.two = {}
            for r, d in ((0, None), (3, 1), (1, 3), (2, 2)):
                if d is not None:
                    self.one[d].wait_recv()
                ref = block_at(self.g, chip(mod4(p1 + r), p2))
                for e in (1, 3, 2):
                    self.two[r, e] = send(ref, ref, to_w=dev(p1, mod4(p2 + e)))
                if self.eager:
                    self.share(ref)

        def third(self):
            for (r, e), op in self.two.items():
                op.wait_recv()
                if self.eager:
                    self.share(block_at(self.g, chip(mod4(p1 + r), mod4(p2 - e))))
            if not self.eager:
                self.share(s.W.at[self.g, :, :, pl.ds(c384, 384)])

        def done(self):
            for op in self.four:
                op.wait_recv()

    gather = {0: Gather(0, True)}
    s.ZS[z] = block[:, 1536:2112]
    stage = [send(s.ZS.at[z], s.ZS.at[z], to_z=to) for to in (zr, zl, zf)]
    gather[1] = Gather(1)
    gather[0].second()
    for op in stage:
        op.wait_recv()
    for k, g in enumerate((4, 5, 6)):
        piece = slice(192 * k, 192 * k + 192)
        two_parts = [s.ZS[2 * c, :, piece], s.ZS[2 * c + 1, :, piece]]
        s.W[g, me, :, pl.ds(c384, 384)] = jnp.concatenate(two_parts, axis=1)
    gather[4] = Gather(4)
    loads[1].wait()
    for t in range(4):
        rows = pl.ds(128 * t, 128)
        seed = jnp.where(s.DC[rows, 0:1] < 8, s.FG[rows, :].astype(F32), 0.0)
        s.FG[rows, :] = seed.astype(BF16)
    loads[0].wait()
    loads[2].wait()

    tile_row = lax.broadcasted_iota(jnp.int32, (128, 128), 0)
    tile_col = lax.broadcasted_iota(jnp.int32, (128, 128), 1)
    for delta in range(2):
        distance = jnp.maximum(128 * delta + tile_row - tile_col, 0)
        bucket = jnp.minimum(distance, 16)
        for edge in bucket_edges:
            bucket = bucket + (distance >= edge).astype(jnp.int32)
        s.BK[delta] = bucket

    gather[0].third()
    gather[4].second()
    gather[1].second()
    for g in (5, 3, 2, 6):
        gather[g] = Gather(g)
    gather[0].done()

    eye = (
        lax.broadcasted_iota(jnp.int32, (8, 256), 0) + 64
        == lax.broadcasted_iota(jnp.int32, (8, 256), 1)
    ).astype(BF16)
    gains = dot_nt(eye, s.W[0, :, :, 512:768].reshape(768, 256))
    s.GN[...] = gains
    last_bias = []
    for h in range(3):
        entry = [gains[3 + h : 4 + h, 24 * k : 24 * k + 1] for k in range(32)]
        last_bias.append(entry[31])
        for delta in range(2):
            bucket = s.BK[delta]
            tile = jnp.broadcast_to(entry[0], (128, 128))
            for k in range(1, 32):
                tile = jnp.where(bucket >= k, entry[k], tile)
            s.T[h, delta] = tile

    for t in range(4):
        rows = pl.ds(128 * t, 128)
        _, unit = norm_parts(s.TOK[rows, :].astype(F32))
        s.FI[rows, :] = (unit * gains[0:1]).astype(BF16)

    def weight(g, start, stop):
        return s.W[g, :, :, start:stop].reshape(768, stop - start)

    query_key = dot(s.FI[...], weight(0, 0, 384))
    for h in range(3):
        s.QH[h] = query_key[:, 64 * h : 64 * h + 64].astype(BF16)
        s.KH[h] = query_key[:, 192 + 64 * h : 256 + 64 * h].astype(BF16)
    value_rows = dot(s.FI[...], weight(0, 384, 576))
    for h in range(3):
        s.VH[h] = value_rows[:, 64 * h : 64 * h + 64].astype(BF16)

    def band(i):
        low = max(0, i - 2)
        return slice(128 * low, 128 * (i + 1)), i - low + 1

    def pack(value):
        return jnp.concatenate([value[0:64], value[64:128]], axis=1)

    def unpack(value):
        return jnp.concatenate([value[:, 0:192], value[:, 192:384]], axis=0)

    class TileSpread:
        def __init__(self, buffer, relay=False):
            self.buffer, self.ops, self.relayed = buffer, {}, relay

        def send(self, k, tile, value):
            self.buffer[z, tile] = pack(value)
            ref = self.buffer.at[z, tile]
            near = (zr, zl) if self.relayed else (zf, zr, zl)
            self.ops[k] = [send(ref, ref, to_z=to) for to in near]

        def relay(self, k):
            from_l, from_r = self.ops[k]
            for op, d, start, to in ((from_l, zl, 0, zr), (from_r, zr, 32, zl)):
                op.wait_recv()
                ref = self.buffer.at[d, k, pl.ds(start, 32)]
                self.ops[k].append(send(ref, ref, to_z=to))
            self.ops[k] = self.ops[k][2:]

        def done(self, k):
            for op in self.ops[k]:
                op.wait_recv()

        def rows(self, tile):
            parts = [self.buffer[k, tile] for k in range(4)]
            top = jnp.concatenate([part[:, 0:192] for part in parts], axis=1)
            bottom = jnp.concatenate([part[:, 192:384] for part in parts], axis=1)
            return jnp.concatenate([top, bottom], axis=0)

    self_spread = TileSpread(s.SMF)
    for i in range(4):
        rows = slice(128 * i, 128 * i + 128)
        keys, count = band(i)
        width = 128 * count
        ahead = lax.broadcasted_iota(jnp.int32, (128, width), 0) - lax.broadcasted_iota(
            jnp.int32, (128, width), 1
        )
        allowed = (s.DC[rows, 0:1] == s.DR[0:1, keys]) & (ahead + 128 * (count - 1) >= 0)
        mixed = []
        for h in range(3):
            tiles = [jnp.broadcast_to(last_bias[h], (128, 128)), s.T[h, 1], s.T[h, 0]][-count:]
            bias = tiles[0] if count == 1 else jnp.concatenate(tiles, axis=1)
            raw = dot_nt(s.QH[h, rows, :], s.KH[h, keys, :])
            probs = softmax(jnp.where(allowed, raw * SCALE + bias, negative))
            s.PS[h, i, :, 0:width] = probs
            mixed.append(dot(probs.astype(BF16), s.VH[h, keys, :]))
        merged = jnp.concatenate(mixed, axis=1).astype(BF16)
        s.SM[rows, :] = merged
        self_spread.send(i, i, merged)
        gather[(5, 3, 2, 6)[i]].second()
    gather[4].third()
    gather[1].third()

    def at(d):
        return pl.ds(mult(128 * d, 128), 128)

    class Scatter:
        made = []

        def __init__(self, part, relay=True):
            n = self.n = len(Scatter.made)
            self.relayed = relay
            self.sends, self.waits = [], []
            self.rows = rows = (pl.ds(0, 64), pl.ds(64, 64))
            Scatter.made.append(self)
            if n >= 2:
                settle(Scatter.made[n - 2].sends)
            slot = n % 2
            if not relay:
                for k, to in enumerate((zf, zr, zl)):
                    s.zsend[slot, k] = part(to).astype(BF16)
                    self.give(s.zsend.at[slot, k], s.zrecv.at[n, k], to)
                s.zown[slot] = part(z)
                return
            s.zsend[slot, 0] = part(zf).astype(BF16)
            for k, to in enumerate((zr, zl)):
                value = part(to)
                first = value[0:64] if k == 0 else value[64:128]
                second = value[64:128] if k == 0 else value[0:64]
                s.ztmp[slot, k] = first
                s.zsend[slot, 1 + k, rows[1 - k]] = second.astype(BF16)
            s.zown[slot] = part(z)

        def start(self):
            n, slot, rows = self.n, self.n % 2, self.rows
            self.relays = [
                self.give(s.zsend.at[slot, 0, rows[k]], s.zrelay.at[n, k], to, False)
                for k, to in enumerate((zr, zl))
            ]
            for k, to in enumerate((zr, zl)):
                self.give(s.zsend.at[slot, 1 + k, rows[1 - k]], s.zrecv.at[n, k, rows[1 - k]], to)

        def give(self, src, dst, to, last=True):
            op = send(src, dst, to_z=to)
            self.sends.append(op)
            if last:
                self.waits.append(op)
            return op

        def middle(self):
            n, slot, rows = self.n, self.n % 2, self.rows
            for k, to in enumerate((zr, zl)):
                self.relays[k].wait_recv()
                total = s.ztmp[slot, k] + s.zrelay[n, k].astype(F32)
                s.zsend[slot, 1 + k, rows[k]] = total.astype(BF16)
                self.give(s.zsend.at[slot, 1 + k, rows[k]], s.zrecv.at[n, k, rows[k]], to)

        def total(self):
            for op in self.waits:
                op.wait_recv()
            total = s.zown[self.n % 2]
            for k in range(2 if self.relayed else 3):
                total = total + s.zrecv[self.n, k].astype(F32)
            return total

    class Spread:
        def __init__(self, ref, relay=True):
            self.ref = ref
            mine = ref.at[at(z)]
            self.ops = [send(mine, mine, to_z=to) for to in ((zr, zl) if relay else (zf, zr, zl))]

        def middle(self):
            from_l, from_r = self.ops
            for op, d, start, to in ((from_l, zl, 0, zr), (from_r, zr, 64, zl)):
                op.wait_recv()
                ref = self.ref.at[pl.ds(mult(128 * d + start, 64), 64)]
                self.ops.append(send(ref, ref, to_z=to))

        def done(self):
            for op in self.ops[2:] if len(self.ops) == 4 else self.ops:
                op.wait_recv()

    def own_heads(g):
        half = s.W[g, :, :, pl.ds(mult(384 * lax.div(z, 2), 128), 384)].reshape(768, 384)
        return jnp.where(lax.rem(z, 2) == 0, half[:, 0:192], half[:, 192:384])

    gather[1].done()
    keys_values = dot(s.MEM[...], weight(1, 0, 384))
    for h in range(3):
        s.CKH[h] = keys_values[:, 64 * h : 64 * h + 64].astype(BF16)
        s.CVH[h] = keys_values[:, 192 + 64 * h : 256 + 64 * h].astype(BF16)
    gather[4].done()
    cross_spread = TileSpread(s.CMF)
    for i in range(4):
        rows = slice(128 * i, 128 * i + 128)
        self_spread.done(i)
        after_self = s.TOK[rows, :].astype(F32) + dot_nt(self_spread.rows(i), weight(4, 0, 768))
        s.AS[rows, :] = after_self
        second_in = (norm_parts(after_self)[1] * s.GN[1:2, :]).astype(BF16)
        s.SI[rows, :] = second_in
        queries = dot(second_in, weight(1, 384, 576)).astype(BF16)
        allowed = s.DC[rows, 0:1] == s.MR[0:1, :]
        mixed = []
        for h in range(3):
            query = queries[:, 64 * h : 64 * h + 64]
            s.CQH[h, rows, :] = query
            raw = dot_nt(query, s.CKH[h])
            probs = softmax(jnp.where(allowed, raw * SCALE, negative))
            s.PC[h, rows, :] = probs
            mixed.append(dot(probs.astype(BF16), s.CVH[h]))
        merged = jnp.concatenate(mixed, axis=1).astype(BF16)
        s.CM[rows, :] = merged
        cross_spread.send(i, i, merged)
        if i == 2:
            gather[5].third()
        if i == 3:
            gather[3].third()
    gather[2].third()
    gather[3].done()
    for t in range(2):
        rows = slice(256 * t, 256 * t + 256)
        s.AGR[rows, :] = dot(s.FG[rows, :], weight(3, 0, 768))
    gather[5].done()

    def cross_merge(tile, rows):
        return s.AS[rows, :] + dot_nt(cross_spread.rows(tile), weight(5, 0, 768))

    for i in range(4):
        rows = slice(128 * i, 128 * i + 128)
        cross_spread.done(i)
        s.TI[rows, :] = (norm_parts(cross_merge(i, rows))[1] * s.GN[2:3, :]).astype(BF16)
    gather[2].done()

    def feed_chunk(d):
        rows = at(d)
        hidden = dot(s.TI[rows, :], weight(2, 0, 768))
        phi = 0.5 + 0.5 * lax.erf(hidden * math.sqrt(0.5))
        slope = phi + hidden * jnp.exp(-0.5 * hidden * hidden) * (1.0 / math.sqrt(2.0 * math.pi))
        s.ACT[rows, :] = (hidden * phi).astype(BF16)
        hidden_grad = (s.AGR[rows, :] * slope).astype(BF16)
        s.HG[rows, :] = hidden_grad
        return dot_nt(hidden_grad, weight(2, 0, 768))

    third_sum = Scatter(feed_chunk, relay=False)

    grad_place = {2: 0, 3: 1, 1: 0, 0: 1}
    held = {}

    def store_grad(g, half, pairs):
        place = grad_place[g]
        if place in held and held[place].g != g and id(held[place].pair) in pending:
            settle([held[place].pair])
        for k in range(2):
            columns = slice(384 * k, 384 * k + 384)
            values = [
                right[columns, :] if left is None else dot_tn(left[:, columns], right).astype(BF16)
                for left, right in pairs
            ]
            value = values[0] if len(values) == 1 else jnp.concatenate(values, axis=1)
            s.GB[place, 8 * k : 8 * k + 8, :, 384 * half : 384 * half + 384] = value.reshape(
                8, 48, 384
            )

    def block_sum(a, b):
        return a.astype(F32) + b.astype(F32)

    class Reduce:
        def __init__(self, g):
            self.g = g
            self.place = grad_place[g]
            self.total = s.HF.at[self.place]
            self.low = s.HB.at[self.place]
            self.pair = send(s.GB.at[self.place, :, :, pl.ds(o384, 384)], s.RB.at[g], to_w=other)

        def first(self):
            g = self.g
            self.pair.wait_recv()
            if self.place in held:
                old = held[self.place]
                settle(list(old.ops.values()))
            held[self.place] = self
            total = block_sum(s.GB[self.place, :, :, pl.ds(c384, 384)], s.RB[g])
            self.total[...] = total
            self.low[...] = total.astype(BF16)
            self.ops = {}
            if g == 0:
                for k, (i, j) in enumerate(plane):
                    xx, yy = mod4(x + i), mod4(y + j)
                    self.ops[k] = send(self.low.at[4 * xx + yy], s.RVS.at[k], to_w=wide_at(xx, yy))
                return
            for e in (1, 3, 2):
                for r in range(4):
                    self.ops[e, r] = send(
                        self.low.at[chip(mod4(p1 + r), mod4(p2 + e))],
                        s.RV.at[g, e - 1, r],
                        to_w=dev(p1, mod4(p2 + e)),
                    )

        def second(self):
            g = self.g
            self.last = {}
            for r in (1, 3, 2, 0):
                total = self.total[chip(mod4(p1 + r), p2)]
                for e in (1, 3, 2):
                    self.ops[e, r].wait_recv()
                    total = total + s.RV[g, e - 1, r].astype(F32)
                if r:
                    s.CB[g, r] = total.astype(BF16)
                    self.last[r] = send(s.CB.at[g, r], s.RCV.at[g, r], to_w=dev(mod4(p1 + r), p2))
                else:
                    self.kept = total

        def third(self):
            g = self.g
            if g == 0:
                total = self.total[4 * x + y]
                for k in range(15):
                    self.ops[k].wait_recv()
                    total = total + s.RVS[k].astype(F32)
            else:
                total = self.kept
                for r in (1, 3, 2):
                    self.last[r].wait_recv()
                    total = total + s.RCV[g, r].astype(F32)
            self.squares = jnp.sum(total * total, axis=0, keepdims=True)
            s.FN[g, 0] = total[0:24]
            s.FN[g, 1] = total[24:48]
            s.RG[g, c] = s.FN[g, c]
            self.give = send(s.FN.at[g, 1 - c], s.RG.at[g, c], to_w=other)

        def done(self):
            self.give.wait_recv()

    def two_halves(g, left, right):
        for half in range(2):
            store_grad(g, half, [(left, right[:, 384 * half : 384 * half + 384])])

    two_halves(2, s.TI, s.HG)
    expand_reduce = Reduce(2)
    feed_sum = Scatter(lambda d: dot_nt(s.ACT[at(d), :], weight(3, 0, 768)))
    feed_sum.start()
    after_cross = cross_merge(z, at(z))
    s.AC[...] = after_cross
    s.M0[...] = own_heads(4)
    two_halves(3, s.FG, s.ACT)
    shrink_reduce = Reduce(3)
    third_grad = third_sum.total()
    cross_path, third_gain = norm_back(s.AC[...], s.GN[2:3, :], third_grad)
    cross_total = s.FG[at(z), :].astype(F32) + cross_path
    cross_out = cross_total.astype(BF16)
    mixed_all = dot(cross_out, weight(5, 0, 768)).astype(BF16)
    for k in range(4):
        s.D4[k] = pack(mixed_all[:, 192 * k : 192 * k + 192])
    s.DMX[z] = s.D4[z]
    mixed_ops = {to: send(s.D4.at[d], s.DMX.at[z], to_z=d) for to, d in enumerate((zr, zl, zf))}
    s.CT[...] = cross_total
    s.COG[at(z), :] = cross_out
    spread = Spread(s.COG)
    gather[6].third()
    expand_reduce.first()
    shrink_reduce.first()
    query_spread = TileSpread(s.DQF, relay=True)
    for op in mixed_ops.values():
        op.wait_recv()

    def cross_back(d):
        rows = slice(128 * d, 128 * d + 128)
        grad = unpack(s.DMX[d])
        parts = []
        for h in range(3):
            mixed_grad = grad[:, 64 * h : 64 * h + 64]
            s.CDMH[h, rows, :] = mixed_grad
            probs_grad = dot_nt(mixed_grad, s.CVH[h])
            probs = s.PC[h, rows, :]
            inner = jnp.sum(probs * probs_grad, axis=-1, keepdims=True)
            raw = (probs * (probs_grad - inner) * SCALE).astype(BF16)
            s.RC[h, rows, :] = raw
            parts.append(dot(raw, s.CKH[h]))
        merged = jnp.concatenate(parts, axis=1).astype(BF16)
        s.DCQ[rows, :] = merged
        query_spread.send(d, d, merged)

    cross_back(3)
    cross_back(2)
    cross_back(1)
    spread.middle()
    cross_back(0)
    query_spread.relay(3)
    parts = [dot_tn(s.RC[h], s.CQH[h]) for h in range(3)]
    parts += [dot_tn(s.PC[h].astype(BF16), s.CDMH[h]) for h in range(3)]
    s.DCKV[...] = jnp.concatenate(parts, axis=1).astype(BF16)
    query_spread.relay(2)
    feed_sum.middle()
    expand_reduce.second()
    query_spread.relay(1)
    store_grad(1, 0, [(s.MEM, s.DCKV[...])])
    query_spread.relay(0)
    memory_sum = Scatter(lambda d: dot_nt(s.DCKV[at(d), :], weight(1, 0, 384)))
    shrink_reduce.second()
    gather[6].done()
    spread.done()
    memory_sum.start()

    s.SOG = s.TI
    for i in (3, 2, 1, 0):
        rows = slice(128 * i, 128 * i + 128)
        query_spread.done(i)
        second_grad = dot_nt(query_spread.rows(i), weight(6, 0, 768))
        self_path, second_gain = norm_back(s.AS[rows, :], s.GN[1:2, :], second_grad)
        s.AS[rows, :] = self_path
        s.GS[i : i + 1, :] = second_gain
        self_out = (s.COG[rows, :].astype(F32) + self_path).astype(BF16)
        s.SOG[rows, :] = self_out
        keys, count = band(i)
        width = 128 * count
        grad = dot(self_out, s.M0[...]).astype(BF16)
        parts = []
        for h in range(3):
            mixed_grad = grad[:, 64 * h : 64 * h + 64]
            s.DMH[h, rows, :] = mixed_grad
            probs_grad = dot_nt(mixed_grad, s.VH[h, keys, :])
            probs = s.PS[h, i, :, 0:width]
            inner = jnp.sum(probs * probs_grad, axis=-1, keepdims=True)
            score_grad = probs * (probs_grad - inner)
            for t in range(count):
                delta = count - 1 - t
                tile = score_grad[:, 128 * t : 128 * t + 128]
                if i == 3:
                    s.AB[h, delta] = tile
                else:
                    s.AB[h, delta] += tile
            raw = (score_grad * SCALE).astype(BF16)
            s.RS[h, i, :, 0:width] = raw
            parts.append(dot(raw, s.KH[h, keys, :]))
        s.DQKV[rows, 0:192] = jnp.concatenate(parts, axis=1).astype(BF16)

        users = range(i, min(i + 2, 3) + 1)
        span = slice(128 * i, 128 * (users[-1] + 1))
        key_parts, value_parts = [], []
        for h in range(3):
            tiles, probs = [], []
            for user in users:
                place = i - max(0, user - 2)
                tiles.append(s.RS[h, user, :, 128 * place : 128 * place + 128])
                probs.append(s.PS[h, user, :, 128 * place : 128 * place + 128].astype(BF16))
            key_parts.append(dot_tn(jnp.concatenate(tiles, axis=0), s.QH[h, span, :]))
            value_parts.append(dot_tn(jnp.concatenate(probs, axis=0), s.DMH[h, span, :]))
        s.DQKV[rows, 192:576] = jnp.concatenate(key_parts + value_parts, axis=1).astype(BF16)

        if i == 2:
            store_grad(1, 1, [(s.SI, s.DCQ[...]), (s.COG, s.CM[...])])
            cross_reduce = Reduce(1)
            expand_reduce.third()
        if i == 1:
            layer_rows = s.AC[...] + feed_sum.total()
            layer_rows = jnp.where(s.DC[at(z), 0:1] < 8, layer_rows, 0.0)
            s.LO[at(z), :] = layer_rows.astype(BF16)
            layer_spread = Spread(s.LO)
            cross_reduce.first()
    shrink_reduce.third()
    s.ST[...] = s.CT[...] + s.AS[at(z), :]
    second_gain = s.GS[pl.ds(z, 1), :]
    first_gains = []

    def first_part(d):
        rows = at(d)
        part = dot_nt(s.DQKV[rows, 0:384], weight(0, 0, 384))
        part = part + dot_nt(s.DQKV[rows, 384:576], weight(0, 384, 576))
        unit = norm_parts(s.TOK[rows, :].astype(F32))[1]
        first_gains.append(jnp.sum(part * unit, axis=0, keepdims=True))
        return part

    first_sum = Scatter(first_part)
    first_sum.start()
    first_gain = sum(first_gains)
    for k in range(2):
        columns = slice(384 * k, 384 * k + 384)
        s.M1[columns, :] = dot_tn(s.SOG[:, columns], s.SM[...]).astype(BF16)
    store_grad(0, 0, [(s.FI, s.DQKV[:, 0:384])])
    store_grad(0, 1, [(s.FI, s.DQKV[:, 384:576]), (None, s.M1)])
    self_reduce = Reduce(0)
    memory_sum.middle()

    for h in range(3):
        for k in range(32):
            total = jnp.zeros((1, 128), F32)
            for delta in range(2):
                chosen = jnp.where(s.BK[delta] == k, s.AB[h, delta], 0.0)
                total = total + jnp.sum(chosen, axis=0, keepdims=True)
            if k == 31:
                total = total + jnp.sum(s.AB[h, 2], axis=0, keepdims=True)
            s.BR[32 * h + k : 32 * h + k + 1, :] = total
    sums = lax.dot_general(
        jnp.ones((8, 128), F32),
        s.BR[...],
        (((1,), (1,)), ((), ())),
        precision=lax.Precision.HIGHEST,
        preferred_element_type=F32,
    )
    self_reduce.first()
    first_sum.middle()

    class Total:
        def __init__(self, buffer, value):
            self.buffer = buffer
            place = 4 * c + z
            buffer[place] = value
            self.ops = [send(buffer.at[place], buffer.at[place], *peer) for peer in chip_line]

        def add(self, start, count):
            for op in self.ops:
                op.wait_recv()
            value = self.buffer[start]
            for k in range(1, count):
                value = value + self.buffer[start + k]
            return value

        def second(self):
            value = self.add(0, 8)
            place = 8 + 4 * x + y
            self.buffer[place] = value
            ref = self.buffer.at[place]
            self.ops = [
                send(ref, ref, to_w=wide_at(mod4(x + i), mod4(y + j))) for i, j in plane
            ]

        def done(self):
            return self.add(8, 16)

    gain_rows = [
        gain[:, 128 * k : 128 * k + 128]
        for gain in (first_gain, second_gain, third_gain)
        for k in range(6)
    ]
    line = jnp.concatenate([sums[0:1, :], jnp.zeros((1, 32), F32)], axis=1)
    bias_rows = [jnp.where(z == k, line, 0.0) for k in range(4)]
    small = jnp.concatenate(gain_rows + bias_rows + [jnp.zeros((2, 128), F32)], axis=0)
    small_sum = Total(s.EX, small)
    layer_spread.middle()
    cross_reduce.second()
    first_grad = first_sum.total()
    token_path, _ = norm_back(s.TOK[at(z), :].astype(F32), s.GN[0:1, :], first_grad)
    s.TG[at(z), :] = (s.ST[...] + token_path).astype(BF16)
    token_spread = Spread(s.TG)
    s.MG[at(z), :] = memory_sum.total().astype(BF16)
    memory_spread = Spread(s.MG)
    small_sum.second()
    memory_spread.middle()
    cross_reduce.third()
    self_reduce.third()
    squares = expand_reduce.squares + shrink_reduce.squares
    squares = squares + cross_reduce.squares + self_reduce.squares
    token_spread.middle()
    norm_sum = Total(s.SC, jnp.broadcast_to(jnp.sum(squares), (8, 128)))
    layer_spread.done()
    move(s.LO, s.lo)
    for op in (expand_reduce, shrink_reduce, cross_reduce):
        op.done()
    small = small_sum.done()
    s.small[...] = small
    small_squares = jnp.sum(small * small)
    norm_sum.second()
    self_reduce.done()
    s.grads[...] = s.RG[...]
    memory_spread.done()
    move(s.MG, s.mg)
    token_spread.done()
    move(s.TG, s.tg)
    last = {id(op) for op in norm_sum.ops}
    settle([op for op in pending.values() if id(op) not in last])
    s.norm[...] = jnp.sqrt(norm_sum.done()[0:1, 0:1] + small_squares)
    settle(list(pending.values()))
    for op in local[3:]:
        op.wait()


def finish(*refs):
    names = ["tlo", "ttg", "tmg", "grads", "small", "tnorm"] + weight_names + output_names
    s = types.SimpleNamespace(**dict(zip(names, refs)))
    w = lax.axis_index("wide")
    z = lax.axis_index("narrow")
    s.lo[...] = s.tlo[...]
    s.tg[...] = s.ttg[...].astype(F32)
    s.mg[...] = s.tmg[...].astype(F32)
    norm = s.tnorm[...]
    s.norm[...] = norm
    factor = clip_norm / jnp.maximum(norm, clip_norm)

    def update(name, index, gradient):
        group = [getattr(s, name + k) for k in "wms"]
        values = [ref[...] if index is None else ref[index] for ref in group]
        new = adamw(*values, gradient, factor, rate_matrix, decay_matrix)
        for k, value in zip("wms", new):
            ref = getattr(s, name + k + "n")
            if index is None:
                ref[...] = value
            else:
                ref[index] = value

    update("s", 0, s.grads[0, 0, :, 0:192])
    update("s", 1, s.grads[0, 0, :, 192:384])
    update("s", 2, s.grads[0, 1, :, 0:192])
    update("m", 0, s.grads[0, 1, :, 192:384])
    update("c", 1, s.grads[1, 0, :, 0:192])
    update("c", 2, s.grads[1, 0, :, 192:384])
    update("c", 0, s.grads[1, 1, :, 0:192])
    update("m", 1, s.grads[1, 1, :, 192:384])
    update("e", None, jnp.concatenate([s.grads[2, 0], s.grads[2, 1]], axis=1))
    update("h", None, jnp.concatenate([s.grads[3, 0], s.grads[3, 1]], axis=1))

    small = s.small[...]
    pick24 = lax.broadcasted_iota(jnp.int32, (768, 128), 0) == 24 * w + lax.broadcasted_iota(
        jnp.int32, (768, 128), 1
    )
    gains = [
        jnp.concatenate([small[6 * k + j : 6 * k + j + 1] for j in range(6)], axis=1)
        for k in range(3)
    ]
    mine = lax.dot_general(
        jnp.concatenate(gains + [jnp.zeros((5, 768), F32)], axis=0),
        pick24.astype(F32),
        (((1,), (0,)), ((), ())),
        precision=lax.Precision.HIGHEST,
        preferred_element_type=F32,
    )
    new = adamw(s.gw[...], s.gm[...], s.gs[...], mine[0:3, 0:24], factor, rate_small, 0.0)
    s.gwn[...], s.gmn[...], s.gsn[...] = new
    row24 = lax.broadcasted_iota(jnp.int32, (24, 128), 0)
    lane = lax.broadcasted_iota(jnp.int32, (24, 128), 1)
    columns = []
    for h in range(3):
        hit = (row24 == 18 + z) & (lane == 32 * h + w)
        columns.append(jnp.sum(jnp.where(hit, small, 0.0)).reshape(1, 1))
    bias_grad = jnp.concatenate(columns, axis=1)
    new = adamw(s.bw[...], s.bm[...], s.bs[...], bias_grad, factor, rate_small, 0.0)
    s.bwn[...], s.bmn[...], s.bsn[...] = new


def shards(*args):
    values = dict(zip(input_names, args))

    def turn(value):
        return jnp.swapaxes(value, -1, -2)

    turned = [part + kind for part in "mhb" for kind in "wms"]
    for name in turned:
        values[name] = turn(values[name])
    any_space = pl.BlockSpec(memory_space=pl.ANY)
    vmem = pl.BlockSpec(memory_space=pltpu.VMEM)
    smem = pl.BlockSpec(memory_space=pltpu.SMEM)
    row_shapes = [jax.ShapeDtypeStruct((512, 768), BF16)] * 3
    shapes = row_shapes + [
        jax.ShapeDtypeStruct((4, 2, 24, 384), F32),
        jax.ShapeDtypeStruct((24, 128), F32),
        jax.ShapeDtypeStruct((1, 1), F32),
    ]
    results = pl.pallas_call(
        kernel,
        out_shape=shapes,
        in_specs=[any_space] * 3 + [smem] * 2 + [vmem] * 7,
        out_specs=[any_space] * 3 + [vmem] * 3,
        scratch_shapes=[pltpu.VMEM(shape, kind) for shape, kind in scratch_shapes.values()]
        + [pltpu.SemaphoreType.DMA((count,)) for count in semaphore_shapes.values()],
        compiler_params=pltpu.CompilerParams(
            collective_id=0, has_side_effects=True, vmem_limit_bytes=62 * 1024 * 1024
        ),
    )(*[values[name] for name in step_inputs])
    shapes = [
        jax.ShapeDtypeStruct((512, 768), BF16),
        jax.ShapeDtypeStruct((512, 768), F32),
        jax.ShapeDtypeStruct((512, 768), F32),
        jax.ShapeDtypeStruct((1, 1), F32),
    ]
    for name in weight_names:
        shapes.append(jax.ShapeDtypeStruct(values[name].shape, F32))
    results = pl.pallas_call(
        finish,
        out_shape=shapes,
        in_specs=[vmem] * (6 + len(weight_names)),
        out_specs=[vmem] * len(shapes),
        compiler_params=pltpu.CompilerParams(vmem_limit_bytes=60 * 1024 * 1024),
    )(*results, *[values[name] for name in weight_names])
    out = dict(zip(output_names, results))
    for name in turned:
        out[name + "n"] = turn(out[name + "n"])
    out["norm"] = out["norm"].reshape(())
    return tuple(out[name] for name in output_names)


def solution(mesh):
    rows = P("wide", None)
    attend = P(None, "wide", "narrow")
    merge = P(None, "narrow", "wide")
    expand = P("wide", "narrow")
    shrink = P("narrow", "wide")
    gains = P(None, "wide")
    weights = (attend,) * 6 + (merge,) * 3 + (expand,) * 3 + (shrink,) * 3 + (gains,) * 3
    weights += (P("narrow", "wide"),) * 3
    in_specs = (rows, rows, rows, P("wide"), P("wide")) + weights
    out_specs = (rows, rows, rows, P()) + weights
    return jax.shard_map(shards, mesh=mesh, in_specs=in_specs, out_specs=out_specs, check_vma=False)
```

```python
import math
import types

import jax
import jax.numpy as jnp
from jax import lax
from jax.experimental import pallas as pl
from jax.experimental.pallas import tpu as pltpu
from jax.sharding import PartitionSpec as P

F32 = jnp.float32
BF16 = jnp.bfloat16
MESH = pl.DeviceIdType.MESH
STEP = 10
bucket_edges = (19, 21, 24, 27, 31, 35, 40, 46, 52, 59, 67, 77, 87, 99, 113)
epsilon = 1e-06
negative = -1e30
beta_one = 0.9
beta_two = 0.999
adam_epsilon = 1e-08
clip_norm = 1.0
rate_matrix = 0.03
rate_small = 1.0
decay_matrix = 0.01
SCALE = 0.125
COPIES = 384

weight_names = [part + kind for part in "scmehgb" for kind in "wms"]
input_names = ["tokens", "memory", "cot", "lens", "mlens"] + weight_names
output_names = ["lo", "tg", "mg", "norm"] + [name + "n" for name in weight_names]
step_inputs = ["tokens", "memory", "cot", "lens", "mlens"] + [part + "w" for part in "scmehgb"]
step_outputs = ["lo", "tg", "mg", "grads", "small", "norm"]

scratch_shapes = dict(
    pk=((2, 24, 2112), F32),
    cat=((2, 24, 2112), F32),
    ZS=((4, 48, 576), BF16),
    W=((7, 16, 48, 768), BF16),
    GN=((8, 768), F32),
    GS=((8, 768), F32),
    DC=((512, 128), jnp.int32),
    DR=((8, 512), jnp.int32),
    MR=((8, 512), jnp.int32),
    TOK=((512, 768), BF16),
    MEM=((512, 768), BF16),
    FG=((512, 768), BF16),
    FI=((512, 768), BF16),
    SI=((512, 768), BF16),
    TI=((512, 768), BF16),
    COG=((512, 768), BF16),
    LO=((512, 768), BF16),
    TG=((512, 768), BF16),
    MG=((512, 768), BF16),
    QH=((3, 512, 64), BF16),
    KH=((3, 512, 64), BF16),
    VH=((3, 512, 64), BF16),
    CQH=((3, 512, 64), BF16),
    CKH=((3, 512, 64), BF16),
    CVH=((3, 512, 64), BF16),
    DMH=((3, 512, 64), BF16),
    CDMH=((3, 512, 64), BF16),
    SM=((512, 192), BF16),
    CM=((512, 192), BF16),
    M0=((768, 192), BF16),
    M1=((768, 192), BF16),
    D4=((4, 64, 384), BF16),
    DMX=((4, 64, 384), BF16),
    SMF=((4, 4, 64, 384), BF16),
    CMF=((4, 4, 64, 384), BF16),
    DQF=((4, 4, 64, 384), BF16),
    T=((3, 2, 128, 128), F32),
    BK=((2, 128, 128), jnp.int32),
    PS=((3, 4, 128, 384), F32),
    PC=((3, 512, 512), F32),
    RS=((3, 4, 128, 384), BF16),
    RC=((3, 512, 512), BF16),
    AGR=((512, 768), F32),
    ACT=((512, 768), BF16),
    HG=((512, 768), BF16),
    DCQ=((512, 192), BF16),
    DCKV=((512, 384), BF16),
    DQKV=((512, 576), BF16),
    AS=((512, 768), F32),
    AC=((128, 768), F32),
    CT=((128, 768), F32),
    ST=((128, 768), F32),
    AB=((3, 3, 128, 128), F32),
    BR=((96, 128), F32),
    zsend=((2, 3, 128, 768), BF16),
    zrelay=((4, 2, 64, 768), BF16),
    zrecv=((4, 3, 128, 768), BF16),
    zown=((3, 128, 768), F32),
    ztmp=((2, 2, 64, 768), F32),
    GB=((2, 16, 48, 768), BF16),
    RB=((4, 16, 48, 384), BF16),
    HF=((2, 16, 48, 384), F32),
    HB=((2, 16, 48, 384), BF16),
    RV=((4, 3, 4, 48, 384), BF16),
    RVS=((15, 48, 384), BF16),
    CB=((4, 4, 48, 384), BF16),
    RCV=((4, 4, 48, 384), BF16),
    FN=((4, 2, 24, 384), F32),
    RG=((4, 2, 24, 384), F32),
    EX=((24, 24, 128), F32),
    SC=((24, 8, 128), F32),
)
semaphore_shapes = dict(ssem=COPIES, rsem=COPIES, lsem=8)


def dot(a, b):
    return jnp.dot(a, b, preferred_element_type=F32)


def dot_nt(a, b):
    return lax.dot_general(a, b, (((1,), (1,)), ((), ())), preferred_element_type=F32)


def dot_tn(a, b):
    return lax.dot_general(a, b, (((0,), (0,)), ((), ())), preferred_element_type=F32)


def mod4(v):
    return lax.rem(v + 4, 4)


def mult(v, n):
    return pl.multiple_of(v, n)


def norm_parts(value):
    scale = lax.rsqrt(jnp.mean(value * value, axis=-1, keepdims=True) + epsilon)
    return scale, value * scale


def norm_back(value, gain_row, grad):
    scale, unit = norm_parts(value)
    gain_grad = jnp.sum(grad * unit, axis=0, keepdims=True)
    inner = grad * gain_row
    value_grad = scale * (inner - unit * jnp.mean(inner * unit, axis=-1, keepdims=True))
    return value_grad, gain_grad


def softmax(scores):
    top = jnp.max(scores, axis=-1, keepdims=True)
    exponent = jnp.exp(scores - top)
    return exponent * (1.0 / jnp.sum(exponent, axis=-1, keepdims=True))


def adamw(weight, moment, square, gradient, factor, rate, decay):
    clipped = gradient * factor
    moment_new = beta_one * moment + (1.0 - beta_one) * clipped
    square_new = beta_two * square + (1.0 - beta_two) * clipped * clipped
    corrected = moment_new / (1.0 - beta_one**STEP)
    scaled = square_new / (1.0 - beta_two**STEP)
    weight_new = weight - rate * (corrected / (jnp.sqrt(scaled) + adam_epsilon) + decay * weight)
    return (weight_new, moment_new, square_new)


def kernel(*refs):
    names = step_inputs + step_outputs + list(scratch_shapes) + list(semaphore_shapes)
    s = types.SimpleNamespace(**dict(zip(names, refs)))
    w = lax.axis_index("wide")
    z = lax.axis_index("narrow")
    c = lax.rem(w, 2)
    y = lax.rem(lax.div(w, 2), 4)
    x = lax.div(w, 8)
    other = w + 1 - 2 * c
    zl, zr, zf = mod4(z - 1), mod4(z + 1), mod4(z + 2)
    p1 = x * (1 - c) + y * c
    p2 = y * (1 - c) + x * c
    s1, s2 = 4 - 3 * c, 1 + 3 * c

    def chip(a, b):
        return s1 * a + s2 * b

    def dev(a, b):
        return 2 * chip(a, b) + c

    def wide_at(xx, yy):
        return (xx * 4 + yy) * 2 + c

    started = []
    pending = {}
    local = []

    def move(src, dst):
        op = pltpu.make_async_copy(src, dst, s.lsem.at[len(local)])
        op.start()
        local.append(op)
        return op

    def settle(ops):
        for op in ops:
            op.wait_send()
            del pending[id(op)]

    def send(src, dst, to_w=None, to_z=None):
        slot = len(started)
        assert slot < COPIES
        op = pltpu.make_async_remote_copy(
            src_ref=src,
            dst_ref=dst,
            send_sem=s.ssem.at[slot],
            recv_sem=s.rsem.at[slot],
            device_id=(w if to_w is None else to_w, z if to_z is None else to_z),
            device_id_type=MESH,
        )
        op.start()
        started.append(op)
        pending[id(op)] = op
        return op

    barrier = pltpu.get_barrier_semaphore()
    plane = [(i, j) for i in range(4) for j in range(4) if (i, j) != (0, 0)]
    chip_line = [(other, z)] + [(to, mod4(z + d)) for d in (1, 3, 2) for to in (w, other)]
    peers = chip_line + [(wide_at(mod4(x + i), mod4(y + j)), z) for i, j in plane]
    for peer in peers:
        pl.semaphore_signal(barrier, inc=1, device_id=peer, device_id_type=MESH)

    loads = [move(s.tokens, s.TOK), move(s.cot, s.FG), move(s.memory, s.MEM)]

    lane = lax.broadcasted_iota(jnp.int32, (24, 128), 1)
    row24 = lax.broadcasted_iota(jnp.int32, (24, 128), 0)
    pick = lax.broadcasted_iota(jnp.int32, (24, 24), 0) == lax.broadcasted_iota(
        jnp.int32, (24, 24), 1
    )
    extra = jnp.zeros((24, 128), F32)
    for k in range(3):
        gain = s.gw[k : k + 1, :]
        column = jnp.sum(jnp.where(pick, gain, 0.0), axis=1, keepdims=True)
        extra = jnp.where(lane == k, column, extra)
        extra = jnp.where((lane == 3 + k) & (row24 == 0), s.bw[0:1, k : k + 1], extra)
    for h in range(2):
        s.pk[h, :, 768:1152] = s.ew[:, 384 * h : 384 * h + 384]
        s.pk[h, :, 1152:1536] = s.hw[:, 384 * h : 384 * h + 384]
        s.pk[h, :, 1536:2112] = jnp.concatenate([s.mw[0], s.mw[1], s.cw[0]], axis=1)
    s.pk[0, :, 0:384] = jnp.concatenate([s.sw[0], s.sw[1]], axis=1)
    s.pk[1, :, 0:384] = jnp.concatenate([s.sw[2], extra, jnp.zeros((24, 64), F32)], axis=1)
    s.pk[0, :, 384:768] = jnp.concatenate([s.cw[1], s.cw[2]], axis=1)
    s.pk[1, :, 384:768] = jnp.concatenate([s.cw[0], jnp.zeros((24, 192), F32)], axis=1)

    pl.semaphore_wait(barrier, len(peers))
    pair = send(s.pk.at[1 - c], s.cat.at[c], to_w=other)
    s.cat[c] = s.pk[c]

    row_col = lax.broadcasted_iota(jnp.int32, (512, 128), 0)
    row_row = lax.broadcasted_iota(jnp.int32, (8, 512), 1)
    doc_col = jnp.zeros((512, 128), jnp.int32)
    doc_row = jnp.zeros((8, 512), jnp.int32)
    mem_row = jnp.zeros((8, 512), jnp.int32)
    end, mem_end = jnp.int32(0), jnp.int32(0)
    for k in range(8):
        end = end + s.lens[k]
        mem_end = mem_end + s.mlens[k]
        doc_col = doc_col + (row_col >= end).astype(jnp.int32)
        doc_row = doc_row + (row_row >= end).astype(jnp.int32)
        mem_row = mem_row + (row_row >= mem_end).astype(jnp.int32)
    s.DC[...] = doc_col
    s.DR[...] = doc_row
    s.MR[...] = jnp.where(mem_row < 8, mem_row, -1)
    pair.wait_recv()
    block = s.cat[...].reshape(48, 2112).astype(BF16)
    me = chip(p1, p2)
    c384 = mult(384 * c, 128)
    o384 = mult(384 * (1 - c), 128)
    for g in range(4):
        s.W[g, me, :, pl.ds(c384, 384)] = block[:, 384 * g : 384 * g + 384]

    def block_at(g, index):
        return s.W.at[g, index, :, pl.ds(c384, 384)]

    class Gather:
        def __init__(self, g, eager=False):
            self.g, self.eager, self.four = g, eager, []
            ref = block_at(g, me)
            self.one = {d: send(ref, ref, to_w=dev(mod4(p1 + d), p2)) for d in (1, 3, 2)}

        def share(self, ref):
            self.four.append(send(ref, ref, to_w=other))

        def second(self):
            self.two = {}
            for r, d in ((0, None), (3, 1), (1, 3), (2, 2)):
                if d is not None:
                    self.one[d].wait_recv()
                ref = block_at(self.g, chip(mod4(p1 + r), p2))
                for e in (1, 3, 2):
                    self.two[r, e] = send(ref, ref, to_w=dev(p1, mod4(p2 + e)))
                if self.eager:
                    self.share(ref)

        def third(self):
            for (r, e), op in self.two.items():
                op.wait_recv()
                if self.eager:
                    self.share(block_at(self.g, chip(mod4(p1 + r), mod4(p2 - e))))
            if not self.eager:
                self.share(s.W.at[self.g, :, :, pl.ds(c384, 384)])

        def done(self):
            for op in self.four:
                op.wait_recv()

    gather = {0: Gather(0, True)}
    s.ZS[z] = block[:, 1536:2112]
    stage = [send(s.ZS.at[z], s.ZS.at[z], to_z=to) for to in (zr, zl, zf)]
    gather[1] = Gather(1)
    gather[0].second()
    for op in stage:
        op.wait_recv()
    for k, g in enumerate((4, 5, 6)):
        piece = slice(192 * k, 192 * k + 192)
        two_parts = [s.ZS[2 * c, :, piece], s.ZS[2 * c + 1, :, piece]]
        s.W[g, me, :, pl.ds(c384, 384)] = jnp.concatenate(two_parts, axis=1)
    gather[4] = Gather(4)
    loads[1].wait()
    for t in range(4):
        rows = pl.ds(128 * t, 128)
        seed = jnp.where(s.DC[rows, 0:1] < 8, s.FG[rows, :].astype(F32), 0.0)
        s.FG[rows, :] = seed.astype(BF16)
    loads[0].wait()
    loads[2].wait()

    tile_row = lax.broadcasted_iota(jnp.int32, (128, 128), 0)
    tile_col = lax.broadcasted_iota(jnp.int32, (128, 128), 1)
    for delta in range(2):
        distance = jnp.maximum(128 * delta + tile_row - tile_col, 0)
        bucket = jnp.minimum(distance, 16)
        for edge in bucket_edges:
            bucket = bucket + (distance >= edge).astype(jnp.int32)
        s.BK[delta] = bucket

    gather[0].third()
    gather[4].second()
    gather[1].second()
    for g in (5, 3, 2, 6):
        gather[g] = Gather(g)
    gather[0].done()

    eye = (
        lax.broadcasted_iota(jnp.int32, (8, 256), 0) + 64
        == lax.broadcasted_iota(jnp.int32, (8, 256), 1)
    ).astype(BF16)
    gains = dot_nt(eye, s.W[0, :, :, 512:768].reshape(768, 256))
    s.GN[...] = gains
    last_bias = []
    for h in range(3):
        entry = [gains[3 + h : 4 + h, 24 * k : 24 * k + 1] for k in range(32)]
        last_bias.append(entry[31])
        for delta in range(2):
            bucket = s.BK[delta]
            tile = jnp.broadcast_to(entry[0], (128, 128))
            for k in range(1, 32):
                tile = jnp.where(bucket >= k, entry[k], tile)
            s.T[h, delta] = tile

    for t in range(4):
        rows = pl.ds(128 * t, 128)
        _, unit = norm_parts(s.TOK[rows, :].astype(F32))
        s.FI[rows, :] = (unit * gains[0:1]).astype(BF16)

    def weight(g, start, stop):
        return s.W[g, :, :, start:stop].reshape(768, stop - start)

    query_key = dot(s.FI[...], weight(0, 0, 384))
    for h in range(3):
        s.QH[h] = query_key[:, 64 * h : 64 * h + 64].astype(BF16)
        s.KH[h] = query_key[:, 192 + 64 * h : 256 + 64 * h].astype(BF16)
    value_rows = dot(s.FI[...], weight(0, 384, 576))
    for h in range(3):
        s.VH[h] = value_rows[:, 64 * h : 64 * h + 64].astype(BF16)

    def band(i):
        low = max(0, i - 2)
        return slice(128 * low, 128 * (i + 1)), i - low + 1

    def pack(value):
        return jnp.concatenate([value[0:64], value[64:128]], axis=1)

    def unpack(value):
        return jnp.concatenate([value[:, 0:192], value[:, 192:384]], axis=0)

    class TileSpread:
        def __init__(self, buffer, relay=False):
            self.buffer, self.ops, self.relayed = buffer, {}, relay

        def send(self, k, tile, value):
            self.buffer[z, tile] = pack(value)
            ref = self.buffer.at[z, tile]
            near = (zr, zl) if self.relayed else (zf, zr, zl)
            self.ops[k] = [send(ref, ref, to_z=to) for to in near]

        def relay(self, k):
            from_l, from_r = self.ops[k]
            for op, d, start, to in ((from_l, zl, 0, zr), (from_r, zr, 32, zl)):
                op.wait_recv()
                ref = self.buffer.at[d, k, pl.ds(start, 32)]
                self.ops[k].append(send(ref, ref, to_z=to))
            self.ops[k] = self.ops[k][2:]

        def done(self, k):
            for op in self.ops[k]:
                op.wait_recv()

        def rows(self, tile):
            parts = [self.buffer[k, tile] for k in range(4)]
            top = jnp.concatenate([part[:, 0:192] for part in parts], axis=1)
            bottom = jnp.concatenate([part[:, 192:384] for part in parts], axis=1)
            return jnp.concatenate([top, bottom], axis=0)

    self_spread = TileSpread(s.SMF)
    for i in range(4):
        rows = slice(128 * i, 128 * i + 128)
        keys, count = band(i)
        width = 128 * count
        ahead = lax.broadcasted_iota(jnp.int32, (128, width), 0) - lax.broadcasted_iota(
            jnp.int32, (128, width), 1
        )
        allowed = (s.DC[rows, 0:1] == s.DR[0:1, keys]) & (ahead + 128 * (count - 1) >= 0)
        mixed = []
        for h in range(3):
            tiles = [jnp.broadcast_to(last_bias[h], (128, 128)), s.T[h, 1], s.T[h, 0]][-count:]
            bias = tiles[0] if count == 1 else jnp.concatenate(tiles, axis=1)
            raw = dot_nt(s.QH[h, rows, :], s.KH[h, keys, :])
            probs = softmax(jnp.where(allowed, raw * SCALE + bias, negative))
            s.PS[h, i, :, 0:width] = probs
            mixed.append(dot(probs.astype(BF16), s.VH[h, keys, :]))
        merged = jnp.concatenate(mixed, axis=1).astype(BF16)
        s.SM[rows, :] = merged
        self_spread.send(i, i, merged)
        gather[(5, 3, 2, 6)[i]].second()
    gather[4].third()
    gather[1].third()

    def at(d):
        return pl.ds(mult(128 * d, 128), 128)

    class Scatter:
        made = []

        def __init__(self, part, relay=True):
            n = self.n = len(Scatter.made)
            self.relayed = relay
            self.sends, self.waits = [], []
            self.rows = rows = (pl.ds(0, 64), pl.ds(64, 64))
            Scatter.made.append(self)
            if n >= 2:
                settle(Scatter.made[n - 2].sends)
            slot = n % 2
            if not relay:
                for k, to in enumerate((zf, zr, zl)):
                    s.zsend[slot, k] = part(to).astype(BF16)
                    self.give(s.zsend.at[slot, k], s.zrecv.at[n, k], to)
                s.zown[slot] = part(z)
                return
            s.zsend[slot, 0] = part(zf).astype(BF16)
            for k, to in enumerate((zr, zl)):
                value = part(to)
                first = value[0:64] if k == 0 else value[64:128]
                second = value[64:128] if k == 0 else value[0:64]
                s.ztmp[slot, k] = first
                s.zsend[slot, 1 + k, rows[1 - k]] = second.astype(BF16)
            s.zown[slot] = part(z)

        def start(self):
            n, slot, rows = self.n, self.n % 2, self.rows
            self.relays = [
                self.give(s.zsend.at[slot, 0, rows[k]], s.zrelay.at[n, k], to, False)
                for k, to in enumerate((zr, zl))
            ]
            for k, to in enumerate((zr, zl)):
                self.give(s.zsend.at[slot, 1 + k, rows[1 - k]], s.zrecv.at[n, k, rows[1 - k]], to)

        def give(self, src, dst, to, last=True):
            op = send(src, dst, to_z=to)
            self.sends.append(op)
            if last:
                self.waits.append(op)
            return op

        def middle(self):
            n, slot, rows = self.n, self.n % 2, self.rows
            for k, to in enumerate((zr, zl)):
                self.relays[k].wait_recv()
                total = s.ztmp[slot, k] + s.zrelay[n, k].astype(F32)
                s.zsend[slot, 1 + k, rows[k]] = total.astype(BF16)
                self.give(s.zsend.at[slot, 1 + k, rows[k]], s.zrecv.at[n, k, rows[k]], to)

        def total(self):
            for op in self.waits:
                op.wait_recv()
            total = s.zown[self.n % 2]
            for k in range(2 if self.relayed else 3):
                total = total + s.zrecv[self.n, k].astype(F32)
            return total

    class Spread:
        def __init__(self, ref, relay=True):
            self.ref = ref
            mine = ref.at[at(z)]
            self.ops = [send(mine, mine, to_z=to) for to in ((zr, zl) if relay else (zf, zr, zl))]

        def middle(self):
            from_l, from_r = self.ops
            for op, d, start, to in ((from_l, zl, 0, zr), (from_r, zr, 64, zl)):
                op.wait_recv()
                ref = self.ref.at[pl.ds(mult(128 * d + start, 64), 64)]
                self.ops.append(send(ref, ref, to_z=to))

        def done(self):
            for op in self.ops[2:] if len(self.ops) == 4 else self.ops:
                op.wait_recv()

    def own_heads(g):
        half = s.W[g, :, :, pl.ds(mult(384 * lax.div(z, 2), 128), 384)].reshape(768, 384)
        return jnp.where(lax.rem(z, 2) == 0, half[:, 0:192], half[:, 192:384])

    gather[1].done()
    keys_values = dot(s.MEM[...], weight(1, 0, 384))
    for h in range(3):
        s.CKH[h] = keys_values[:, 64 * h : 64 * h + 64].astype(BF16)
        s.CVH[h] = keys_values[:, 192 + 64 * h : 256 + 64 * h].astype(BF16)
    gather[4].done()
    cross_spread = TileSpread(s.CMF)
    for i in range(4):
        rows = slice(128 * i, 128 * i + 128)
        self_spread.done(i)
        after_self = s.TOK[rows, :].astype(F32) + dot_nt(self_spread.rows(i), weight(4, 0, 768))
        s.AS[rows, :] = after_self
        second_in = (norm_parts(after_self)[1] * s.GN[1:2, :]).astype(BF16)
        s.SI[rows, :] = second_in
        queries = dot(second_in, weight(1, 384, 576)).astype(BF16)
        allowed = s.DC[rows, 0:1] == s.MR[0:1, :]
        mixed = []
        for h in range(3):
            query = queries[:, 64 * h : 64 * h + 64]
            s.CQH[h, rows, :] = query
            raw = dot_nt(query, s.CKH[h])
            probs = softmax(jnp.where(allowed, raw * SCALE, negative))
            s.PC[h, rows, :] = probs
            mixed.append(dot(probs.astype(BF16), s.CVH[h]))
        merged = jnp.concatenate(mixed, axis=1).astype(BF16)
        s.CM[rows, :] = merged
        cross_spread.send(i, i, merged)
        if i == 2:
            gather[5].third()
        if i == 3:
            gather[3].third()
    gather[2].third()
    gather[3].done()
    for t in range(2):
        rows = slice(256 * t, 256 * t + 256)
        s.AGR[rows, :] = dot(s.FG[rows, :], weight(3, 0, 768))
    gather[5].done()

    def cross_merge(tile, rows):
        return s.AS[rows, :] + dot_nt(cross_spread.rows(tile), weight(5, 0, 768))

    for i in range(4):
        rows = slice(128 * i, 128 * i + 128)
        cross_spread.done(i)
        s.TI[rows, :] = (norm_parts(cross_merge(i, rows))[1] * s.GN[2:3, :]).astype(BF16)
    gather[2].done()

    def feed_chunk(d):
        rows = at(d)
        hidden = dot(s.TI[rows, :], weight(2, 0, 768))
        phi = 0.5 + 0.5 * lax.erf(hidden * math.sqrt(0.5))
        slope = phi + hidden * jnp.exp(-0.5 * hidden * hidden) * (1.0 / math.sqrt(2.0 * math.pi))
        s.ACT[rows, :] = (hidden * phi).astype(BF16)
        hidden_grad = (s.AGR[rows, :] * slope).astype(BF16)
        s.HG[rows, :] = hidden_grad
        return dot_nt(hidden_grad, weight(2, 0, 768))

    third_sum = Scatter(feed_chunk, relay=False)

    grad_place = {2: 0, 3: 1, 1: 0, 0: 1}
    held = {}

    def store_grad(g, half, pairs):
        place = grad_place[g]
        if place in held and held[place].g != g and id(held[place].pair) in pending:
            settle([held[place].pair])
        for k in range(2):
            columns = slice(384 * k, 384 * k + 384)
            values = [
                right[columns, :] if left is None else dot_tn(left[:, columns], right).astype(BF16)
                for left, right in pairs
            ]
            value = values[0] if len(values) == 1 else jnp.concatenate(values, axis=1)
            s.GB[place, 8 * k : 8 * k + 8, :, 384 * half : 384 * half + 384] = value.reshape(
                8, 48, 384
            )

    def block_sum(a, b):
        return a.astype(F32) + b.astype(F32)

    class Reduce:
        def __init__(self, g):
            self.g = g
            self.place = grad_place[g]
            self.total = s.HF.at[self.place]
            self.low = s.HB.at[self.place]
            self.pair = send(s.GB.at[self.place, :, :, pl.ds(o384, 384)], s.RB.at[g], to_w=other)

        def first(self):
            g = self.g
            self.pair.wait_recv()
            if self.place in held:
                old = held[self.place]
                settle(list(old.ops.values()))
            held[self.place] = self
            total = block_sum(s.GB[self.place, :, :, pl.ds(c384, 384)], s.RB[g])
            self.total[...] = total
            self.low[...] = total.astype(BF16)
            self.ops = {}
            if g == 0:
                for k, (i, j) in enumerate(plane):
                    xx, yy = mod4(x + i), mod4(y + j)
                    self.ops[k] = send(self.low.at[4 * xx + yy], s.RVS.at[k], to_w=wide_at(xx, yy))
                return
            for e in (1, 3, 2):
                for r in range(4):
                    self.ops[e, r] = send(
                        self.low.at[chip(mod4(p1 + r), mod4(p2 + e))],
                        s.RV.at[g, e - 1, r],
                        to_w=dev(p1, mod4(p2 + e)),
                    )

        def second(self):
            g = self.g
            self.last = {}
            for r in (1, 3, 2, 0):
                total = self.total[chip(mod4(p1 + r), p2)]
                for e in (1, 3, 2):
                    self.ops[e, r].wait_recv()
                    total = total + s.RV[g, e - 1, r].astype(F32)
                if r:
                    s.CB[g, r] = total.astype(BF16)
                    self.last[r] = send(s.CB.at[g, r], s.RCV.at[g, r], to_w=dev(mod4(p1 + r), p2))
                else:
                    self.kept = total

        def third(self):
            g = self.g
            if g == 0:
                total = self.total[4 * x + y]
                for k in range(15):
                    self.ops[k].wait_recv()
                    total = total + s.RVS[k].astype(F32)
            else:
                total = self.kept
                for r in (1, 3, 2):
                    self.last[r].wait_recv()
                    total = total + s.RCV[g, r].astype(F32)
            self.squares = jnp.sum(total * total, axis=0, keepdims=True)
            s.FN[g, 0] = total[0:24]
            s.FN[g, 1] = total[24:48]
            s.RG[g, c] = s.FN[g, c]
            self.give = send(s.FN.at[g, 1 - c], s.RG.at[g, c], to_w=other)

        def done(self):
            self.give.wait_recv()

    def two_halves(g, left, right):
        for half in range(2):
            store_grad(g, half, [(left, right[:, 384 * half : 384 * half + 384])])

    two_halves(2, s.TI, s.HG)
    expand_reduce = Reduce(2)
    feed_sum = Scatter(lambda d: dot_nt(s.ACT[at(d), :], weight(3, 0, 768)))
    feed_sum.start()
    after_cross = cross_merge(z, at(z))
    s.AC[...] = after_cross
    s.M0[...] = own_heads(4)
    two_halves(3, s.FG, s.ACT)
    shrink_reduce = Reduce(3)
    third_grad = third_sum.total()
    cross_path, third_gain = norm_back(s.AC[...], s.GN[2:3, :], third_grad)
    cross_total = s.FG[at(z), :].astype(F32) + cross_path
    cross_out = cross_total.astype(BF16)
    mixed_all = dot(cross_out, weight(5, 0, 768)).astype(BF16)
    for k in range(4):
        s.D4[k] = pack(mixed_all[:, 192 * k : 192 * k + 192])
    s.DMX[z] = s.D4[z]
    mixed_ops = {to: send(s.D4.at[d], s.DMX.at[z], to_z=d) for to, d in enumerate((zr, zl, zf))}
    s.CT[...] = cross_total
    s.COG[at(z), :] = cross_out
    spread = Spread(s.COG)
    gather[6].third()
    expand_reduce.first()
    shrink_reduce.first()
    query_spread = TileSpread(s.DQF, relay=True)
    for op in mixed_ops.values():
        op.wait_recv()

    def cross_back(d):
        rows = slice(128 * d, 128 * d + 128)
        grad = unpack(s.DMX[d])
        parts = []
        for h in range(3):
            mixed_grad = grad[:, 64 * h : 64 * h + 64]
            s.CDMH[h, rows, :] = mixed_grad
            probs_grad = dot_nt(mixed_grad, s.CVH[h])
            probs = s.PC[h, rows, :]
            inner = jnp.sum(probs * probs_grad, axis=-1, keepdims=True)
            raw = (probs * (probs_grad - inner) * SCALE).astype(BF16)
            s.RC[h, rows, :] = raw
            parts.append(dot(raw, s.CKH[h]))
        merged = jnp.concatenate(parts, axis=1).astype(BF16)
        s.DCQ[rows, :] = merged
        query_spread.send(d, d, merged)

    cross_back(3)
    cross_back(2)
    cross_back(1)
    spread.middle()
    cross_back(0)
    query_spread.relay(3)
    parts = [dot_tn(s.RC[h], s.CQH[h]) for h in range(3)]
    parts += [dot_tn(s.PC[h].astype(BF16), s.CDMH[h]) for h in range(3)]
    s.DCKV[...] = jnp.concatenate(parts, axis=1).astype(BF16)
    query_spread.relay(2)
    feed_sum.middle()
    expand_reduce.second()
    query_spread.relay(1)
    store_grad(1, 0, [(s.MEM, s.DCKV[...])])
    query_spread.relay(0)
    memory_sum = Scatter(lambda d: dot_nt(s.DCKV[at(d), :], weight(1, 0, 384)))
    shrink_reduce.second()
    gather[6].done()
    spread.done()
    memory_sum.start()

    s.SOG = s.TI
    for i in (3, 2, 1, 0):
        rows = slice(128 * i, 128 * i + 128)
        query_spread.done(i)
        second_grad = dot_nt(query_spread.rows(i), weight(6, 0, 768))
        self_path, second_gain = norm_back(s.AS[rows, :], s.GN[1:2, :], second_grad)
        s.AS[rows, :] = self_path
        s.GS[i : i + 1, :] = second_gain
        self_out = (s.COG[rows, :].astype(F32) + self_path).astype(BF16)
        s.SOG[rows, :] = self_out
        keys, count = band(i)
        width = 128 * count
        grad = dot(self_out, s.M0[...]).astype(BF16)
        parts = []
        for h in range(3):
            mixed_grad = grad[:, 64 * h : 64 * h + 64]
            s.DMH[h, rows, :] = mixed_grad
            probs_grad = dot_nt(mixed_grad, s.VH[h, keys, :])
            probs = s.PS[h, i, :, 0:width]
            inner = jnp.sum(probs * probs_grad, axis=-1, keepdims=True)
            score_grad = probs * (probs_grad - inner)
            for t in range(count):
                delta = count - 1 - t
                tile = score_grad[:, 128 * t : 128 * t + 128]
                if i == 3:
                    s.AB[h, delta] = tile
                else:
                    s.AB[h, delta] += tile
            raw = (score_grad * SCALE).astype(BF16)
            s.RS[h, i, :, 0:width] = raw
            parts.append(dot(raw, s.KH[h, keys, :]))
        s.DQKV[rows, 0:192] = jnp.concatenate(parts, axis=1).astype(BF16)

        users = range(i, min(i + 2, 3) + 1)
        span = slice(128 * i, 128 * (users[-1] + 1))
        key_parts, value_parts = [], []
        for h in range(3):
            tiles, probs = [], []
            for user in users:
                place = i - max(0, user - 2)
                tiles.append(s.RS[h, user, :, 128 * place : 128 * place + 128])
                probs.append(s.PS[h, user, :, 128 * place : 128 * place + 128].astype(BF16))
            key_parts.append(dot_tn(jnp.concatenate(tiles, axis=0), s.QH[h, span, :]))
            value_parts.append(dot_tn(jnp.concatenate(probs, axis=0), s.DMH[h, span, :]))
        s.DQKV[rows, 192:576] = jnp.concatenate(key_parts + value_parts, axis=1).astype(BF16)

        if i == 2:
            store_grad(1, 1, [(s.SI, s.DCQ[...]), (s.COG, s.CM[...])])
            cross_reduce = Reduce(1)
            expand_reduce.third()
        if i == 1:
            layer_rows = s.AC[...] + feed_sum.total()
            layer_rows = jnp.where(s.DC[at(z), 0:1] < 8, layer_rows, 0.0)
            s.LO[at(z), :] = layer_rows.astype(BF16)
            layer_spread = Spread(s.LO)
            cross_reduce.first()
    shrink_reduce.third()
    s.ST[...] = s.CT[...] + s.AS[at(z), :]
    second_gain = s.GS[pl.ds(z, 1), :]
    first_gains = []

    def first_part(d):
        rows = at(d)
        part = dot_nt(s.DQKV[rows, 0:384], weight(0, 0, 384))
        part = part + dot_nt(s.DQKV[rows, 384:576], weight(0, 384, 576))
        unit = norm_parts(s.TOK[rows, :].astype(F32))[1]
        first_gains.append(jnp.sum(part * unit, axis=0, keepdims=True))
        return part

    first_sum = Scatter(first_part)
    first_sum.start()
    first_gain = sum(first_gains)
    for k in range(2):
        columns = slice(384 * k, 384 * k + 384)
        s.M1[columns, :] = dot_tn(s.SOG[:, columns], s.SM[...]).astype(BF16)
    store_grad(0, 0, [(s.FI, s.DQKV[:, 0:384])])
    store_grad(0, 1, [(s.FI, s.DQKV[:, 384:576]), (None, s.M1)])
    self_reduce = Reduce(0)
    memory_sum.middle()

    for h in range(3):
        for k in range(32):
            total = jnp.zeros((1, 128), F32)
            for delta in range(2):
                chosen = jnp.where(s.BK[delta] == k, s.AB[h, delta], 0.0)
                total = total + jnp.sum(chosen, axis=0, keepdims=True)
            if k == 31:
                total = total + jnp.sum(s.AB[h, 2], axis=0, keepdims=True)
            s.BR[32 * h + k : 32 * h + k + 1, :] = total
    sums = lax.dot_general(
        jnp.ones((8, 128), F32),
        s.BR[...],
        (((1,), (1,)), ((), ())),
        precision=lax.Precision.HIGHEST,
        preferred_element_type=F32,
    )
    self_reduce.first()
    first_sum.middle()

    class Total:
        def __init__(self, buffer, value):
            self.buffer = buffer
            place = 4 * c + z
            buffer[place] = value
            self.ops = [send(buffer.at[place], buffer.at[place], *peer) for peer in chip_line]

        def add(self, start, count):
            for op in self.ops:
                op.wait_recv()
            value = self.buffer[start]
            for k in range(1, count):
                value = value + self.buffer[start + k]
            return value

        def second(self):
            value = self.add(0, 8)
            place = 8 + 4 * x + y
            self.buffer[place] = value
            ref = self.buffer.at[place]
            self.ops = [
                send(ref, ref, to_w=wide_at(mod4(x + i), mod4(y + j))) for i, j in plane
            ]

        def done(self):
            return self.add(8, 16)

    gain_rows = [
        gain[:, 128 * k : 128 * k + 128]
        for gain in (first_gain, second_gain, third_gain)
        for k in range(6)
    ]
    line = jnp.concatenate([sums[0:1, :], jnp.zeros((1, 32), F32)], axis=1)
    bias_rows = [jnp.where(z == k, line, 0.0) for k in range(4)]
    small = jnp.concatenate(gain_rows + bias_rows + [jnp.zeros((2, 128), F32)], axis=0)
    small_sum = Total(s.EX, small)
    s.MG[at(z), :] = memory_sum.total().astype(BF16)
    memory_spread = Spread(s.MG)
    layer_spread.middle()
    cross_reduce.second()
    first_grad = first_sum.total()
    token_path, _ = norm_back(s.TOK[at(z), :].astype(F32), s.GN[0:1, :], first_grad)
    s.TG[at(z), :] = (s.ST[...] + token_path).astype(BF16)
    token_spread = Spread(s.TG)
    small_sum.second()
    memory_spread.middle()
    cross_reduce.third()
    self_reduce.third()
    squares = expand_reduce.squares + shrink_reduce.squares
    squares = squares + cross_reduce.squares + self_reduce.squares
    token_spread.middle()
    norm_sum = Total(s.SC, jnp.broadcast_to(jnp.sum(squares), (8, 128)))
    layer_spread.done()
    move(s.LO, s.lo)
    for op in (expand_reduce, shrink_reduce, cross_reduce):
        op.done()
    small = small_sum.done()
    s.small[...] = small
    small_squares = jnp.sum(small * small)
    norm_sum.second()
    self_reduce.done()
    s.grads[...] = s.RG[...]
    memory_spread.done()
    move(s.MG, s.mg)
    token_spread.done()
    move(s.TG, s.tg)
    last = {id(op) for op in norm_sum.ops}
    settle([op for op in pending.values() if id(op) not in last])
    s.norm[...] = jnp.sqrt(norm_sum.done()[0:1, 0:1] + small_squares)
    settle(list(pending.values()))
    for op in local[3:]:
        op.wait()


def finish(*refs):
    names = ["tlo", "ttg", "tmg", "grads", "small", "tnorm"] + weight_names + output_names
    s = types.SimpleNamespace(**dict(zip(names, refs)))
    w = lax.axis_index("wide")
    z = lax.axis_index("narrow")
    s.lo[...] = s.tlo[...]
    s.tg[...] = s.ttg[...].astype(F32)
    s.mg[...] = s.tmg[...].astype(F32)
    norm = s.tnorm[...]
    s.norm[...] = norm
    factor = clip_norm / jnp.maximum(norm, clip_norm)

    def update(name, index, gradient):
        group = [getattr(s, name + k) for k in "wms"]
        values = [ref[...] if index is None else ref[index] for ref in group]
        new = adamw(*values, gradient, factor, rate_matrix, decay_matrix)
        for k, value in zip("wms", new):
            ref = getattr(s, name + k + "n")
            if index is None:
                ref[...] = value
            else:
                ref[index] = value

    update("s", 0, s.grads[0, 0, :, 0:192])
    update("s", 1, s.grads[0, 0, :, 192:384])
    update("s", 2, s.grads[0, 1, :, 0:192])
    update("m", 0, s.grads[0, 1, :, 192:384])
    update("c", 1, s.grads[1, 0, :, 0:192])
    update("c", 2, s.grads[1, 0, :, 192:384])
    update("c", 0, s.grads[1, 1, :, 0:192])
    update("m", 1, s.grads[1, 1, :, 192:384])
    update("e", None, jnp.concatenate([s.grads[2, 0], s.grads[2, 1]], axis=1))
    update("h", None, jnp.concatenate([s.grads[3, 0], s.grads[3, 1]], axis=1))

    small = s.small[...]
    pick24 = lax.broadcasted_iota(jnp.int32, (768, 128), 0) == 24 * w + lax.broadcasted_iota(
        jnp.int32, (768, 128), 1
    )
    gains = [
        jnp.concatenate([small[6 * k + j : 6 * k + j + 1] for j in range(6)], axis=1)
        for k in range(3)
    ]
    mine = lax.dot_general(
        jnp.concatenate(gains + [jnp.zeros((5, 768), F32)], axis=0),
        pick24.astype(F32),
        (((1,), (0,)), ((), ())),
        precision=lax.Precision.HIGHEST,
        preferred_element_type=F32,
    )
    new = adamw(s.gw[...], s.gm[...], s.gs[...], mine[0:3, 0:24], factor, rate_small, 0.0)
    s.gwn[...], s.gmn[...], s.gsn[...] = new
    row24 = lax.broadcasted_iota(jnp.int32, (24, 128), 0)
    lane = lax.broadcasted_iota(jnp.int32, (24, 128), 1)
    columns = []
    for h in range(3):
        hit = (row24 == 18 + z) & (lane == 32 * h + w)
        columns.append(jnp.sum(jnp.where(hit, small, 0.0)).reshape(1, 1))
    bias_grad = jnp.concatenate(columns, axis=1)
    new = adamw(s.bw[...], s.bm[...], s.bs[...], bias_grad, factor, rate_small, 0.0)
    s.bwn[...], s.bmn[...], s.bsn[...] = new


def shards(*args):
    values = dict(zip(input_names, args))

    def turn(value):
        return jnp.swapaxes(value, -1, -2)

    turned = [part + kind for part in "mhb" for kind in "wms"]
    for name in turned:
        values[name] = turn(values[name])
    any_space = pl.BlockSpec(memory_space=pl.ANY)
    vmem = pl.BlockSpec(memory_space=pltpu.VMEM)
    smem = pl.BlockSpec(memory_space=pltpu.SMEM)
    row_shapes = [jax.ShapeDtypeStruct((512, 768), BF16)] * 3
    shapes = row_shapes + [
        jax.ShapeDtypeStruct((4, 2, 24, 384), F32),
        jax.ShapeDtypeStruct((24, 128), F32),
        jax.ShapeDtypeStruct((1, 1), F32),
    ]
    results = pl.pallas_call(
        kernel,
        out_shape=shapes,
        in_specs=[any_space] * 3 + [smem] * 2 + [vmem] * 7,
        out_specs=[any_space] * 3 + [vmem] * 3,
        scratch_shapes=[pltpu.VMEM(shape, kind) for shape, kind in scratch_shapes.values()]
        + [pltpu.SemaphoreType.DMA((count,)) for count in semaphore_shapes.values()],
        compiler_params=pltpu.CompilerParams(
            collective_id=0, has_side_effects=True, vmem_limit_bytes=62 * 1024 * 1024
        ),
    )(*[values[name] for name in step_inputs])
    shapes = [
        jax.ShapeDtypeStruct((512, 768), BF16),
        jax.ShapeDtypeStruct((512, 768), F32),
        jax.ShapeDtypeStruct((512, 768), F32),
        jax.ShapeDtypeStruct((1, 1), F32),
    ]
    for name in weight_names:
        shapes.append(jax.ShapeDtypeStruct(values[name].shape, F32))
    results = pl.pallas_call(
        finish,
        out_shape=shapes,
        in_specs=[vmem] * (6 + len(weight_names)),
        out_specs=[vmem] * len(shapes),
        compiler_params=pltpu.CompilerParams(vmem_limit_bytes=60 * 1024 * 1024),
    )(*results, *[values[name] for name in weight_names])
    out = dict(zip(output_names, results))
    for name in turned:
        out[name + "n"] = turn(out[name + "n"])
    out["norm"] = out["norm"].reshape(())
    return tuple(out[name] for name in output_names)


def solution(mesh):
    rows = P("wide", None)
    attend = P(None, "wide", "narrow")
    merge = P(None, "narrow", "wide")
    expand = P("wide", "narrow")
    shrink = P("narrow", "wide")
    gains = P(None, "wide")
    weights = (attend,) * 6 + (merge,) * 3 + (expand,) * 3 + (shrink,) * 3 + (gains,) * 3
    weights += (P("narrow", "wide"),) * 3
    in_specs = (rows, rows, rows, P("wide"), P("wide")) + weights
    out_specs = (rows, rows, rows, P()) + weights
    return jax.shard_map(shards, mesh=mesh, in_specs=in_specs, out_specs=out_specs, check_vma=False)
```
